32 devices in a mesh: ctx: 16 (over z, y, core), ch: 2 (over x).
Axes of the slice: x: 2, y: 2, z: 4, core: 2. Of those that a mesh axis runs over, the one named last changes fastest.
Arguments:
- activations: bfloat16 [2, 2048, 8192], P(None, 'ctx', 'ch'), may hold values from -62 to 62
- grad_in: bfloat16 [2, 2048, 8192], P(None, 'ctx', 'ch'), may hold values from -6 to 6
- gate_out: bfloat16 [3, 2, 2048, 8192], P(None, None, 'ctx', 'ch'), may hold values from -6 to 6
- gate_in: bfloat16 [3, 2, 2048, 8192], P(None, None, 'ctx', 'ch'), may hold values from -6 to 6
- filters: bfloat16 [3, 512, 128], P(None, 'ch'), may hold values from -0.5 to 0.5
Outputs:
- grad_input: bfloat16 [2, 2048, 8192], P(None, 'ctx', 'ch')
- grad_gate_out: bfloat16 [3, 2, 2048, 8192], P(None, None, 'ctx', 'ch')
- grad_gate_in: bfloat16 [3, 2, 2048, 8192], P(None, None, 'ctx', 'ch')
- grad_filters: float32 [3, 512, 128], P(None, 'ch', 'ctx')
The draws below stay inside these ranges and needn't reach their ends.
All inputs are finite; a program needn't handle non-finite values.
Results may differ from the reference program's by a relative error of at most 0.023.
Values may be sent and summed in bfloat16 or wider, within the bound.
No kernel may reach another device: no remote copies, remote signals or barrier semaphores. Data moves between devices by JAX's collectives and lax.ppermute only.
A program may use at most 256 MiB of HBM per device.

```python
import math
import jax
import jax.numpy as jnp
from jax import lax

D = 8192
GROUP = 16
FL = 128
SEQS = 2
LAYERS = 3
LENGTH = 2048
GROUPS = 512
N_CTX = 16


def draw_activations(key, part):
    keys = jax.random.split(jax.random.fold_in(key, 11), 3)
    row_scale = jnp.exp(jax.random.uniform(keys[0], (SEQS, LENGTH, 1), jnp.float32) * math.log(10.0))
    col_scale = jnp.exp(jnp.linspace(0.0, math.log(3.0), D, dtype=jnp.float32) + jax.random.uniform(keys[1], (D,), jnp.float32) * math.log(3.4))
    base = jnp.clip(jax.random.normal(keys[2], (SEQS, LENGTH, D), jnp.float32), -6.0, 6.0)
    return (base * row_scale * col_scale / 10.0).astype(jnp.bfloat16)


def block_scale(stream_key, extent, shards, smallest, largest):
    def one(dim, parts):
        heights = jax.random.uniform(jax.random.fold_in(jax.random.fold_in(stream_key, 6), dim), (parts,), jnp.float32, smallest / len(shards), largest / len(shards))
        return jnp.repeat(jnp.exp(heights), extent[dim] // parts).reshape((-1,) + (1,) * (len(extent) - dim - 1))

    level = one(*shards[0])
    for cut in shards[1:]:
        level = level * one(*cut)
    return level


def bell_draw(key, dims, scale, bound, pieces=(), kind=jnp.bfloat16):
    entries = scale * jax.random.normal(key, dims, jnp.float32)
    if pieces:
        entries = entries * block_scale(key, dims, pieces, -0.22, 0.18)
    return jnp.clip(entries, -bound, bound).astype(kind)


def setup_inputs(seed: int = 0) -> dict:
    key_list = jax.random.split(jax.random.key(seed), 6)
    return {
        "activations": draw_activations(jax.random.fold_in(key_list[5], 71), 0),
        "grad_in": bell_draw(key_list[1], (SEQS, LENGTH, D), 1.0, 6.0, ((1, 16), (2, 2))),
        "gate_out": bell_draw(key_list[2], (LAYERS, SEQS, LENGTH, D), 1.0, 6.0, ((2, 16), (3, 2))),
        "gate_in": bell_draw(key_list[3], (LAYERS, SEQS, LENGTH, D), 1.0, 6.0, ((2, 16), (3, 2))),
        "filters": bell_draw(key_list[4], (LAYERS, GROUPS, FL), FL ** -0.5, 0.5, ((1, 2),)),
    }


def rows_of(folded):
    seq_count, length_all, width_all = folded.shape
    block_rows = length_all // (2 * N_CTX)
    blocks = folded.reshape(seq_count, N_CTX, 2, block_rows, width_all)
    leading = blocks[:, :, 0]
    trailing = blocks[:, ::-1, 1]
    return jnp.concatenate([leading, trailing], axis=1).reshape(seq_count, length_all, width_all)

def folded_of(ordered):
    seq_count, length_all, width_all = ordered.shape
    block_rows = length_all // (2 * N_CTX)
    blocks = ordered.reshape(seq_count, 2 * N_CTX, block_rows, width_all)
    leading = blocks[:, :N_CTX]
    trailing = blocks[:, N_CTX:][:, ::-1]
    return jnp.stack([leading, trailing], axis=2).reshape(seq_count, length_all, width_all)

def spread_taps(taps_group):
    return jnp.repeat(taps_group, GROUP, axis=0).T

def causal_filter(signal, spread):
    length_all = signal.shape[1]
    fft_size = length_all + FL
    spectrum = jnp.fft.rfft(signal, fft_size, axis=1) * jnp.fft.rfft(spread, fft_size, axis=0)[None]
    return jnp.fft.irfft(spectrum, fft_size, axis=1)[:, :length_all]

def reverse_filter(signal, spread):
    length_all = signal.shape[1]
    fft_size = length_all + FL
    spectrum = jnp.fft.rfft(signal, fft_size, axis=1) * jnp.conj(jnp.fft.rfft(spread, fft_size, axis=0))[None]
    return jnp.fft.irfft(spectrum, fft_size, axis=1)[:, :length_all]

def lag_sums(gradient, signal):
    length_all = signal.shape[1]
    fft_size = length_all + FL
    spectrum = jnp.conj(jnp.fft.rfft(signal, fft_size, axis=1)) * jnp.fft.rfft(gradient, fft_size, axis=1)
    lagged = jnp.fft.irfft(spectrum, fft_size, axis=1)[:, :FL]
    summed = lax.optimization_barrier(jnp.sum(lagged, axis=0))
    return lax.optimization_barrier(jnp.sum(summed.reshape(FL, GROUPS, GROUP), axis=2)).T

def reference(activations, grad_in, gate_out, gate_in, filters):
    current = activations
    saved = []
    for layer_index in range(LAYERS):
        spread = spread_taps(filters[layer_index].astype(jnp.float32))
        values = current.astype(jnp.float32)
        inverse_rms = lax.rsqrt(lax.optimization_barrier(jnp.mean(values * values, axis=2, keepdims=True)) + 1e-06)
        normed = values * inverse_rms
        inputs = (gate_in[layer_index].astype(jnp.float32) * normed).astype(jnp.bfloat16)
        inputs = lax.optimization_barrier(inputs)
        filtered = causal_filter(inputs.astype(jnp.float32), spread)
        saved.append((spread, inverse_rms, normed, inputs, filtered))
        current = (gate_out[layer_index].astype(jnp.float32) * filtered).astype(jnp.bfloat16)
        current = lax.optimization_barrier(current)
    gradient = rows_of(grad_in)
    out_grads = []
    in_grads = []
    filter_grads = []
    for layer_index in reversed(range(LAYERS)):
        spread, inverse_rms, normed, inputs, filtered = saved[layer_index]
        incoming = gradient.astype(jnp.float32)
        out_grads.append((incoming * filtered).astype(jnp.bfloat16))
        gated = (gate_out[layer_index].astype(jnp.float32) * incoming).astype(jnp.bfloat16)
        gated = lax.optimization_barrier(gated)
        gated_float = gated.astype(jnp.float32)
        spread_back = reverse_filter(gated_float, spread)
        filter_grads.append(lag_sums(gated_float, inputs.astype(jnp.float32)))
        in_grads.append((spread_back * normed).astype(jnp.bfloat16))
        grad_normed = spread_back * gate_in[layer_index].astype(jnp.float32)
        inner = lax.optimization_barrier(jnp.mean(grad_normed * normed, axis=2, keepdims=True))
        gradient = (inverse_rms * (grad_normed - normed * inner)).astype(jnp.bfloat16)
        gradient = lax.optimization_barrier(gradient)
    return (folded_of(gradient), jnp.stack(out_grads[::-1]), jnp.stack(in_grads[::-1]), jnp.stack(filter_grads[::-1]))
```

```python
import functools

import jax
import jax.numpy as jnp
from jax import lax
from jax.experimental import pallas as pl
from jax.experimental.pallas import tpu as pltpu
from jax.sharding import PartitionSpec as P

D = 8192
GROUP = 16
LAYERS = 3
EPS = 1e-06
LANES = 128
SUB = 8
BLOCK = 512
VMEM_LIMIT = 48 * 1024 * 1024

f32 = jnp.float32
bf16 = jnp.bfloat16


def down_rows(row):
    count = row.shape[1]
    return jnp.broadcast_to(row, (count, count)).T


def lane_sums(acc):
    return jnp.broadcast_to(jnp.sum(acc.T, axis=0, keepdims=True), (SUB, acc.shape[0]))


def lag_flip(taps):
    row = lax.broadcasted_iota(jnp.int32, (taps, taps), 0)
    col = lax.broadcasted_iota(jnp.int32, (taps, taps), 1)
    return (lax.rem(row + col, taps) == 0).astype(bf16)


def band(taps_row, half, behind):
    taps = taps_row.shape[1]
    wheel = pltpu.roll(
        jnp.broadcast_to(taps_row, (half, taps)), 0, 1, stride=1, stride_axis=0
    )
    row = lax.broadcasted_iota(jnp.int32, (half, taps), 0)
    col = lax.broadcasted_iota(jnp.int32, (half, taps), 1)
    first = (col > row) if behind else (col >= row)
    zero = jnp.zeros_like(wheel)
    return jnp.concatenate(
        [jnp.where(first, wheel, zero), jnp.where(first, zero, wheel)], axis=1
    ).astype(bf16)


def windows(signal, half):
    shifted_up = jnp.concatenate([signal[half:], signal[:half]], axis=0)
    return jnp.concatenate([signal, shifted_up], axis=1)


def group_pick(stacked, half):
    count = LANES // GROUP
    owner = lax.broadcasted_iota(jnp.int32, (half, LANES), 1) // GROUP
    parts = []
    for side in range(2):
        picked = stacked[:half, side * LANES : (side + 1) * LANES]
        for g in range(1, count):
            piece = stacked[g * half : (g + 1) * half, side * LANES : (side + 1) * LANES]
            picked = jnp.where(owner == g, piece, picked)
        parts.append(picked)
    return jnp.concatenate(parts, axis=0)


def filtered_block(taps_rows, signal, behind):
    half = signal.shape[0] // 4
    count = LANES // GROUP
    bands = jnp.concatenate(
        [band(taps_rows[g : g + 1], half, behind) for g in range(count)], axis=0
    )
    stacked = jnp.dot(bands, windows(signal, half), preferred_element_type=f32)
    return group_pick(stacked, half)


def lanes_of(index):
    return slice(index * LANES, (index + 1) * LANES)


def groups_of(index):
    count = LANES // GROUP
    return slice(index * count, (index + 1) * count)


def scale_of(total_ref):
    return down_rows(lax.rsqrt(total_ref[0:1, :] / D + EPS))


def enter_kernel(x_ref, gate_ref, v_ref, ssq_ref, acc_ref):
    step = pl.program_id(0)

    @pl.when(step == 0)
    def _():
        acc_ref[...] = jnp.zeros_like(acc_ref)

    for sub in range(x_ref.shape[1] // LANES):
        at = lanes_of(sub)
        values = x_ref[:, at].astype(f32)
        acc_ref[...] += values * values
        v_ref[:, at] = (gate_ref[:, at].astype(f32) * values).astype(bf16)

    @pl.when(step == pl.num_programs(0) - 1)
    def _():
        ssq_ref[...] = lane_sums(acc_ref[...])


def forward_kernel(
    taps_ref, own_ref, halo_ref, own_tot_ref, halo_tot_ref, gate_out_ref, gate_in_ref,
    z_ref, x_ref, v_ref, ssq_ref, own_scale, halo_scale, acc_ref,
):
    step = pl.program_id(0)

    @pl.when(step == 0)
    def _():
        own_scale[...] = scale_of(own_tot_ref)
        halo_scale[...] = scale_of(halo_tot_ref)
        acc_ref[...] = jnp.zeros_like(acc_ref)

    taps = jnp.dot(taps_ref[...], lag_flip(taps_ref.shape[1]), preferred_element_type=f32)
    for sub in range(own_ref.shape[1] // LANES):
        at = lanes_of(sub)
        signal = jnp.concatenate(
            [
                (halo_ref[:, at].astype(f32) * halo_scale[...]).astype(bf16),
                (own_ref[:, at].astype(f32) * own_scale[...]).astype(bf16),
            ],
            axis=0,
        )
        z = filtered_block(taps[groups_of(sub)], signal, True)
        z_ref[:, at] = z.astype(bf16)
        x = (gate_out_ref[:, at].astype(f32) * z).astype(bf16)
        x_ref[:, at] = x
        values = x.astype(f32)
        acc_ref[...] += values * values
        v_ref[:, at] = (gate_in_ref[:, at].astype(f32) * values).astype(bf16)

    @pl.when(step == pl.num_programs(0) - 1)
    def _():
        ssq_ref[...] = lane_sums(acc_ref[...])


def last_forward_kernel(
    taps_ref, own_ref, halo_ref, own_tot_ref, halo_tot_ref, top_ref, bottom_ref, *rest
):
    out_ref, own_scale, halo_scale = rest[-3:]
    step = pl.program_id(0)

    @pl.when(step == 0)
    def _():
        own_scale[...] = scale_of(own_tot_ref)
        halo_scale[...] = scale_of(halo_tot_ref)

    taps = jnp.dot(taps_ref[...], lag_flip(taps_ref.shape[1]), preferred_element_type=f32)
    for sub in range(own_ref.shape[1] // LANES):
        at = lanes_of(sub)
        signal = jnp.concatenate(
            [
                (halo_ref[:, at].astype(f32) * halo_scale[...]).astype(bf16),
                (own_ref[:, at].astype(f32) * own_scale[...]).astype(bf16),
            ],
            axis=0,
        )
        z = filtered_block(taps[groups_of(sub)], signal, True)
        gradient = jnp.concatenate([top_ref[:, at], bottom_ref[:, at]], axis=0).astype(f32)
        out_ref[:, at] = (gradient * z).astype(bf16)


def gate_kernel(top_ref, bottom_ref, gate_ref, gz_ref):
    half = top_ref.shape[0]
    gz_ref[:half] = (top_ref[...].astype(f32) * gate_ref[:half].astype(f32)).astype(bf16)
    gz_ref[half:] = (bottom_ref[...].astype(f32) * gate_ref[half:].astype(f32)).astype(bf16)


def backward_kernel(taps_ref, own_ref, halo_ref, tot_ref, x_ref, gate_ref, *rest):
    out_ref, gn_ref, inner_ref, scale, acc_ref = rest[-5:]
    step = pl.program_id(0)

    @pl.when(step == 0)
    def _():
        scale[...] = scale_of(tot_ref)
        acc_ref[...] = jnp.zeros_like(acc_ref)

    taps = taps_ref[...].astype(f32)
    for sub in range(own_ref.shape[1] // LANES):
        at = lanes_of(sub)
        signal = jnp.concatenate([own_ref[:, at], halo_ref[:, at]], axis=0)
        gu = filtered_block(taps[groups_of(sub)], signal, False)
        normed = x_ref[:, at].astype(f32) * scale[...]
        out_ref[:, at] = (gu * normed).astype(bf16)
        gn = gu * gate_ref[:, at].astype(f32)
        gn_ref[:, at] = gn.astype(bf16)
        acc_ref[...] += gn * normed

    @pl.when(step == pl.num_programs(0) - 1)
    def _():
        inner_ref[...] = lane_sums(acc_ref[...])


def input_gradient(gn_ref, x_ref, at, scale, mean):
    normed = x_ref[:, at].astype(f32) * scale[...]
    return (scale[...] * (gn_ref[:, at].astype(f32) - normed * mean[...])).astype(bf16)


def between_kernel(gn_ref, x_ref, tot_ref, inner_ref, z_ref, gate_ref, *rest):
    out_ref, gz_ref, scale, mean = rest[-4:]

    @pl.when(pl.program_id(0) == 0)
    def _():
        scale[...] = scale_of(tot_ref)
        mean[...] = down_rows(inner_ref[0:1, :] / D)

    for sub in range(x_ref.shape[1] // LANES):
        at = lanes_of(sub)
        gradient = input_gradient(gn_ref, x_ref, at, scale, mean).astype(f32)
        gz_ref[:, at] = (gate_ref[:, at].astype(f32) * gradient).astype(bf16)
        out_ref[:, at] = (gradient * z_ref[:, at].astype(f32)).astype(bf16)


def finish_kernel(gn_ref, x_ref, tot_ref, inner_ref, top_ref, bottom_ref, scale, mean):
    half = top_ref.shape[0]

    @pl.when(pl.program_id(0) == 0)
    def _():
        scale[...] = scale_of(tot_ref)
        mean[...] = down_rows(inner_ref[0:1, :] / D)

    for sub in range(x_ref.shape[1] // LANES):
        at = lanes_of(sub)
        gradient = input_gradient(gn_ref, x_ref, at, scale, mean)
        top_ref[:, at] = gradient[:half]
        bottom_ref[:, at] = gradient[half:]


def fold_kernel(odd_ref, first_ref, second_ref, *rest):
    out_ref = rest[-1]
    half = first_ref.shape[0]
    odd = odd_ref[0]

    @pl.when(odd == 0)
    def _():
        out_ref[:half] = first_ref[...]
        out_ref[half:] = second_ref[...]

    @pl.when(odd != 0)
    def _():
        out_ref[:half] = second_ref[...]
        out_ref[half:] = first_ref[...]


def taps_kernel(*refs):
    ins, (out_ref, flipped, scales) = refs[:-3], refs[-3:]
    per = 5
    seqs = len(ins) // per
    rows = ins[0].shape[0]
    half = rows // 2
    count = LANES // GROUP

    @pl.when(pl.program_id(0) == 0)
    def _():
        for s in range(seqs):
            scales[2 * s] = scale_of(ins[per * s + 3])
            scales[2 * s + 1] = scale_of(ins[per * s + 4])

    owner = lax.broadcasted_iota(jnp.int32, (half, LANES), 1) // GROUP
    row = lax.broadcasted_iota(jnp.int32, (half, LANES), 0)
    col = lax.broadcasted_iota(jnp.int32, (half, LANES), 1)
    masks = [(owner == g).astype(bf16) for g in range(count)]
    for sub in range(ins[0].shape[1] // LANES):
        at = lanes_of(sub)
        grads = []
        signals = []
        for s in range(seqs):
            gz_ref, own_ref, halo_ref = ins[per * s : per * s + 3]
            grads += [gz_ref[:half, at], gz_ref[half:, at]]
            signal = jnp.concatenate(
                [
                    (halo_ref[:, at].astype(f32) * scales[2 * s + 1]).astype(bf16),
                    (own_ref[:, at].astype(f32) * scales[2 * s]).astype(bf16),
                ],
                axis=0,
            )
            signals.append(windows(signal, half))
        wide = jnp.concatenate(grads, axis=1)
        left = jnp.concatenate(
            [wide * jnp.concatenate([masks[g]] * len(grads), axis=1) for g in range(count)],
            axis=0,
        )
        products = lax.dot_general(
            left,
            jnp.concatenate(signals, axis=1),
            (((1,), (1,)), ((), ())),
            preferred_element_type=f32,
        )
        slabs = []
        for g in range(count):
            mine = products[g * half : (g + 1) * half]
            wheel = jnp.where(col > row, mine[:, :LANES], mine[:, LANES:])
            slab = wheel[:SUB]
            for a in range(SUB, half, SUB):
                slab = slab + pltpu.roll(wheel[a : a + SUB], LANES - a, 1)
            slabs.append(slab)
        slabs = jnp.concatenate(slabs, axis=0)
        within = lax.rem(lax.broadcasted_iota(jnp.int32, slabs.shape, 0), SUB)
        for bit in (1, 2, 4):
            turned = pltpu.roll(slabs, LANES - bit, 1)
            slabs = jnp.where(within & bit != 0, turned, slabs)
        flipped[groups_of(sub), :] = jnp.sum(slabs.reshape(count, SUB, LANES), axis=1)
    out_ref[...] = jnp.dot(
        flipped[...].astype(bf16), lag_flip(out_ref.shape[1]), preferred_element_type=f32
    ).astype(bf16)


class Calls:
    def __init__(self, rows, width, taps):
        self.rows, self.width, self.taps = rows, width, taps
        self.half = rows // 2
        self.block = min(BLOCK, width)
        self.steps = width // self.block

    def flat(self, array, s=None, layer=None, rows=None):
        rows = self.rows if rows is None else rows
        lead = tuple(i for i in (layer, s) if i is not None)
        spec = pl.BlockSpec(
            (None,) * len(lead) + (rows, self.block), lambda j, *_: lead + (0, j)
        )
        return array, spec

    def small(self, array=None):
        return array, pl.BlockSpec((SUB, self.rows), lambda j, *_: (0, 0))

    def filters(self, array, layer):
        count = self.block // GROUP
        return array, pl.BlockSpec((None, count, self.taps), lambda j, *_: (layer, j, 0))

    def square(self):
        return pltpu.VMEM((self.rows, self.rows), f32)

    def call(self, kernel, name, ins, outs, scratch=(), carry=None, work=1.0, prefetch=()):
        operands = [a for a, _ in ins]
        in_specs = [b for _, b in ins]
        aliases = {}
        if carry is not None:
            aliases = {len(prefetch) + len(operands): 0}
            operands.append(carry)
            in_specs.append(pl.BlockSpec(memory_space=pl.ANY))
        return pl.pallas_call(
            kernel,
            name=name,
            out_shape=[jax.ShapeDtypeStruct(s, d) for s, d, _ in outs],
            grid_spec=pltpu.PrefetchScalarGridSpec(
                num_scalar_prefetch=len(prefetch),
                grid=(self.steps,),
                in_specs=in_specs,
                out_specs=[b for _, _, b in outs],
                scratch_shapes=list(scratch),
            ),
            input_output_aliases=aliases,
            compiler_params=pltpu.CompilerParams(
                dimension_semantics=("arbitrary",), vmem_limit_bytes=VMEM_LIMIT
            ),
            cost_estimate=pl.CostEstimate(
                flops=int(work * 1e9), bytes_accessed=int(work * 3e6), transcendentals=0
            ),
        )(*prefetch, *operands)


def shifted(value, steps):
    count = lax.axis_size("ctx")
    first, last = max(0, -steps), min(count, count - steps)
    return lax.ppermute(value, "ctx", [(r, r + steps) for r in range(first, last)])


def over_channels(value):
    if lax.axis_size("ch") == 2:
        return value + lax.ppermute(value, "ch", [(0, 1), (1, 0)])
    return lax.psum(value, "ch")


def owner_routes(count):
    blocks = [[], []]
    for block in range(2 * count):
        folded = block if block < count else 2 * count - 1 - block
        blocks[block % 2].append((folded, block // 2))
    return blocks


def local(activations, grad_in, gate_out, gate_in, filters):
    seqs, rows, width = activations.shape
    taps = filters.shape[2]
    assert rows == taps == LANES
    half = rows // 2
    c = Calls(rows, width, taps)
    one = ((rows, width), bf16, c.flat(None)[1])
    part = ((half, width), bf16, c.flat(None, rows=half)[1])
    vector = ((SUB, rows), f32, c.small()[1])
    routes = owner_routes(lax.axis_size("ctx"))
    odd = lax.rem(lax.axis_index("ctx"), 2)

    arrived = []
    for side in range(2):
        start = jnp.where(odd == side, 0, half)
        piece = lax.dynamic_slice_in_dim(grad_in, start, half, axis=1)
        arrived.append(lax.ppermute(piece, "ctx", routes[side]))

    x = [[None] * seqs for _ in range(LAYERS)]
    z = [[None] * seqs for _ in range(LAYERS)]
    own = [[None] * seqs for _ in range(LAYERS)]
    halo = [[None] * seqs for _ in range(LAYERS)]
    own_tot = [[None] * seqs for _ in range(LAYERS)]
    halo_tot = [[None] * seqs for _ in range(LAYERS)]

    def send(layer, s, v, ssq):
        own[layer][s] = v
        halo[layer][s] = shifted(v, 1)
        own_tot[layer][s] = over_channels(ssq)
        halo_tot[layer][s] = shifted(own_tot[layer][s], 1)

    for s in range(seqs):
        x[0][s] = c.flat(activations, s)
        v, ssq = c.call(
            enter_kernel, "enter", [x[0][s], c.flat(gate_in, s, 0)], [one, vector],
            [c.square()],
        )
        send(0, s, v, ssq)

    def signal_of(layer, s):
        return [
            c.flat(own[layer][s]), c.flat(halo[layer][s]),
            c.small(own_tot[layer][s]), c.small(halo_tot[layer][s]),
        ]

    for layer in range(LAYERS - 1):
        for s in range(seqs):
            z[layer][s], nx, v, ssq = c.call(
                forward_kernel, "forward",
                [c.filters(filters, layer)] + signal_of(layer, s)
                + [c.flat(gate_out, s, layer), c.flat(gate_in, s, layer + 1)],
                [one, one, one, vector],
                [c.square()] * 3, work=3.0,
            )
            x[layer + 1][s] = c.flat(nx)
            send(layer + 1, s, v, ssq)

    last = LAYERS - 1
    gz = [[None] * seqs for _ in range(LAYERS)]
    gz_halo = [[None] * seqs for _ in range(LAYERS)]
    for s in range(seqs):
        (gz[last][s],) = c.call(
            gate_kernel, "gate",
            [c.flat(arrived[0], s, rows=half), c.flat(arrived[1], s, rows=half),
             c.flat(gate_out, s, last)],
            [one],
        )
        gz_halo[last][s] = shifted(gz[last][s], -1)

    whole = (gate_out.shape, bf16)
    out_grads = in_grads = None
    for s in range(seqs):
        (out_grads,) = c.call(
            last_forward_kernel, "last_forward",
            [c.filters(filters, last)] + signal_of(last, s)
            + [c.flat(arrived[0], s, rows=half), c.flat(arrived[1], s, rows=half)],
            [whole + (c.flat(None, s, last)[1],)],
            [c.square()] * 2, carry=out_grads, work=3.0,
        )

    def taps_of(layer):
        ins = []
        for s in range(seqs):
            ins += [c.flat(gz[layer][s])] + signal_of(layer, s)
        count = c.block // GROUP
        (found,) = c.call(
            taps_kernel, "taps", ins,
            [((width // GROUP, taps), bf16, pl.BlockSpec((count, taps), lambda j: (j, 0)))],
            [pltpu.VMEM((count, taps), f32), pltpu.VMEM((2 * seqs, rows, rows), f32)],
            work=6.0,
        )
        return found

    found = [None] * LAYERS
    returned = [[None, None] for _ in range(seqs)]
    for layer in reversed(range(LAYERS)):
        found[layer] = taps_of(layer)
        for s in range(seqs):
            in_grads, gn, inner = c.call(
                backward_kernel, "backward",
                [c.filters(filters, layer), c.flat(gz[layer][s]), c.flat(gz_halo[layer][s]),
                 c.small(own_tot[layer][s]), x[layer][s], c.flat(gate_in, s, layer)],
                [whole + (c.flat(None, s, layer)[1],), one, vector],
                [c.square()] * 2, carry=in_grads, work=3.0,
            )
            common = [
                c.flat(gn), x[layer][s], c.small(own_tot[layer][s]),
                c.small(over_channels(inner)),
            ]
            if layer:
                out_grads, gz[layer - 1][s] = c.call(
                    between_kernel, "between",
                    common + [c.flat(z[layer - 1][s]), c.flat(gate_out, s, layer - 1)],
                    [whole + (c.flat(None, s, layer - 1)[1],), one],
                    [c.square()] * 2, carry=out_grads,
                )
                gz_halo[layer - 1][s] = shifted(gz[layer - 1][s], -1)
            else:
                halves = c.call(
                    finish_kernel, "finish", common, [part, part], [c.square()] * 2
                )
                for side in range(2):
                    back = [(d, r) for r, d in routes[side]]
                    returned[s][side] = lax.ppermute(halves[side], "ctx", back)

    grad_filters = lax.psum_scatter(
        jnp.stack(found), "ctx", scatter_dimension=2, tiled=True
    ).astype(f32)

    grad_input = None
    for s in range(seqs):
        (grad_input,) = c.call(
            fold_kernel, "fold",
            [c.flat(returned[s][0], rows=half), c.flat(returned[s][1], rows=half)],
            [(activations.shape, bf16, c.flat(None, s)[1])],
            carry=grad_input, prefetch=(odd.reshape(1).astype(jnp.int32),),
        )
    return grad_input, out_grads, in_grads, grad_filters


def solution(mesh):
    return jax.shard_map(
        local,
        mesh=mesh,
        in_specs=(
            P(None, "ctx", "ch"),
            P(None, "ctx", "ch"),
            P(None, None, "ctx", "ch"),
            P(None, None, "ctx", "ch"),
            P(None, "ch", None),
        ),
        out_specs=(
            P(None, "ctx", "ch"),
            P(None, None, "ctx", "ch"),
            P(None, None, "ctx", "ch"),
            P(None, "ch", "ctx"),
        ),
        check_vma=False,
    )
```

```python
import functools

import jax
import jax.numpy as jnp
from jax import lax
from jax.experimental import pallas as pl
from jax.experimental.pallas import tpu as pltpu
from jax.sharding import PartitionSpec as P

D = 8192
GROUP = 16
LAYERS = 3
EPS = 1e-06
LANES = 128
SUB = 8
BLOCK = 1024
HEIGHT = 32
VMEM_LIMIT = 20 * 1024 * 1024

f32 = jnp.float32
bf16 = jnp.bfloat16


def down_rows(row):
    count = row.shape[1]
    return jnp.broadcast_to(row, (count, count)).T


def lane_sums(acc):
    return jnp.broadcast_to(jnp.sum(acc.T, axis=0, keepdims=True), (SUB, acc.shape[0]))


def lag_flip(taps):
    row = lax.broadcasted_iota(jnp.int32, (taps, taps), 0)
    col = lax.broadcasted_iota(jnp.int32, (taps, taps), 1)
    return (lax.rem(row + col, taps) == 0).astype(bf16)


def band_masks(height, taps, behind):
    row = lax.broadcasted_iota(jnp.int32, (height, taps), 0)
    col = lax.broadcasted_iota(jnp.int32, (height, taps), 1)
    first = (col > row) if behind else (col >= row)
    return jnp.concatenate(
        [jnp.where(first, 1.0, 0.0), jnp.where(first, 0.0, 1.0)], axis=1
    ).astype(bf16)


def band(taps_row, masks):
    height, taps = masks.shape[0], taps_row.shape[1]
    wheel = pltpu.roll(
        jnp.broadcast_to(taps_row, (height, taps)), 0, 1, stride=1, stride_axis=0
    ).astype(bf16)
    return jnp.concatenate([wheel, wheel], axis=1) * masks


def windows(signal, height):
    count = signal.shape[0] // 2 // height
    return jnp.concatenate(
        [signal]
        + [
            jnp.concatenate([signal[k * height :], signal[: k * height]], axis=0)
            for k in range(1, count)
        ],
        axis=1,
    )


def group_pick(stacked, height, sides):
    count = LANES // GROUP
    owner = lax.broadcasted_iota(jnp.int32, (height, LANES), 1) // GROUP
    parts = []
    for side in range(sides):
        at = lanes_of(side)
        picked = stacked[:height, at]
        for g in range(1, count):
            picked = jnp.where(owner == g, stacked[g * height : (g + 1) * height, at], picked)
        parts.append(picked)
    return jnp.concatenate(parts, axis=0)


def filtered_block(taps_rows, signal, masks):
    height = masks.shape[0]
    count = LANES // GROUP
    bands = jnp.concatenate([band(taps_rows[g : g + 1], masks) for g in range(count)], axis=0)
    stacked = jnp.dot(bands, windows(signal, height), preferred_element_type=f32)
    return group_pick(stacked, height, signal.shape[0] // 2 // height)


def lanes_of(index):
    return slice(index * LANES, (index + 1) * LANES)


def groups_of(index):
    count = LANES // GROUP
    return slice(index * count, (index + 1) * count)


def scale_of(total_ref):
    return down_rows(lax.rsqrt(total_ref[0:1, :] / D + EPS))


def squares_kernel(x_ref, ssq_ref, acc_ref):
    step = pl.program_id(0)

    @pl.when(step == 0)
    def _():
        acc_ref[...] = jnp.zeros_like(acc_ref)

    for s in range(x_ref.shape[0]):
        for sub in range(x_ref.shape[2] // LANES):
            values = x_ref[s, :, lanes_of(sub)].astype(f32)
            acc_ref[s] += values * values

    @pl.when(step == pl.num_programs(0) - 1)
    def _():
        for s in range(x_ref.shape[0]):
            ssq_ref[s * SUB : (s + 1) * SUB] = lane_sums(acc_ref[s])


def input_kernel(x_ref, tot_ref, gate_ref, *rest):
    u_ref, scale = rest[-2:]

    @pl.when(pl.program_id(0) == 0)
    def _():
        scale[...] = scale_of(tot_ref)

    for sub in range(x_ref.shape[1] // LANES):
        at = lanes_of(sub)
        normed = x_ref[:, at].astype(f32) * scale[...]
        u_ref[:, at] = (gate_ref[:, at].astype(f32) * normed).astype(bf16)


def behind_block(taps, own_ref, halo_ref, sub, masks):
    at = lanes_of(sub)
    signal = jnp.concatenate([halo_ref[:, at], own_ref[:, at]], axis=0)
    return filtered_block(taps[groups_of(sub)], signal, masks)


def flipped_taps(taps_ref):
    return jnp.dot(taps_ref[...], lag_flip(taps_ref.shape[1]), preferred_element_type=f32)


def forward_kernel(taps_ref, own_ref, halo_ref, gate_ref, *rest):
    z_ref, x_ref, ssq_ref, acc_ref = rest[-4:]
    step = pl.program_id(0)

    @pl.when(step == 0)
    def _():
        acc_ref[...] = jnp.zeros_like(acc_ref)

    taps = flipped_taps(taps_ref)
    masks = band_masks(HEIGHT, taps.shape[1], True)
    for sub in range(own_ref.shape[1] // LANES):
        at = lanes_of(sub)
        z = behind_block(taps, own_ref, halo_ref, sub, masks)
        z_ref[:, at] = z.astype(bf16)
        x = (gate_ref[:, at].astype(f32) * z).astype(bf16)
        x_ref[:, at] = x
        values = x.astype(f32)
        acc_ref[...] += values * values

    @pl.when(step == pl.num_programs(0) - 1)
    def _():
        ssq_ref[...] = lane_sums(acc_ref[...])


def last_forward_kernel(taps_ref, own_ref, halo_ref, top_ref, bottom_ref, *rest):
    out_ref = rest[-1]
    taps = flipped_taps(taps_ref)
    masks = band_masks(HEIGHT, taps.shape[1], True)
    for sub in range(own_ref.shape[1] // LANES):
        at = lanes_of(sub)
        z = behind_block(taps, own_ref, halo_ref, sub, masks)
        gradient = jnp.concatenate([top_ref[:, at], bottom_ref[:, at]], axis=0).astype(f32)
        out_ref[:, at] = (gradient * z).astype(bf16)


def gate_kernel(top_ref, bottom_ref, gate_ref, *rest):
    gz_ref = rest[-1]
    half = top_ref.shape[0]
    gz_ref[:half] = (top_ref[...].astype(f32) * gate_ref[:half].astype(f32)).astype(bf16)
    gz_ref[half:] = (bottom_ref[...].astype(f32) * gate_ref[half:].astype(f32)).astype(bf16)


def backward_kernel(taps_ref, own_ref, halo_ref, tot_ref, x_ref, gate_ref, *rest):
    out_ref, gn_ref, inner_ref, scale, acc_ref = rest[-5:]
    step = pl.program_id(0)

    @pl.when(step == 0)
    def _():
        scale[...] = scale_of(tot_ref)
        acc_ref[...] = jnp.zeros_like(acc_ref)

    taps = taps_ref[...].astype(f32)
    masks = band_masks(HEIGHT, taps.shape[1], False)
    for sub in range(own_ref.shape[1] // LANES):
        at = lanes_of(sub)
        signal = jnp.concatenate([own_ref[:, at], halo_ref[:, at]], axis=0)
        gu = filtered_block(taps[groups_of(sub)], signal, masks)
        normed = x_ref[:, at].astype(f32) * scale[...]
        out_ref[:, at] = (gu * normed).astype(bf16)
        gn = gu * gate_ref[:, at].astype(f32)
        gn_ref[:, at] = gn.astype(bf16)
        acc_ref[...] += gn * normed

    @pl.when(step == pl.num_programs(0) - 1)
    def _():
        inner_ref[...] = lane_sums(acc_ref[...])


def input_gradient(gn_ref, x_ref, at, scale, mean):
    normed = x_ref[:, at].astype(f32) * scale[...]
    return (scale[...] * (gn_ref[:, at].astype(f32) - normed * mean[...])).astype(bf16)


def between_kernel(gn_ref, x_ref, tot_ref, inner_ref, z_ref, gate_ref, *rest):
    out_ref, gz_ref, scale, mean = rest[-4:]

    @pl.when(pl.program_id(0) == 0)
    def _():
        scale[...] = scale_of(tot_ref)
        mean[...] = down_rows(inner_ref[0:1, :] / D)

    for sub in range(x_ref.shape[1] // LANES):
        at = lanes_of(sub)
        gradient = input_gradient(gn_ref, x_ref, at, scale, mean).astype(f32)
        gz_ref[:, at] = (gate_ref[:, at].astype(f32) * gradient).astype(bf16)
        out_ref[:, at] = (gradient * z_ref[:, at].astype(f32)).astype(bf16)


def finish_kernel(gn_ref, x_ref, tot_ref, inner_ref, *rest):
    top_ref, bottom_ref, scale, mean = rest[-4:]
    half = top_ref.shape[0]

    @pl.when(pl.program_id(0) == 0)
    def _():
        scale[...] = scale_of(tot_ref)
        mean[...] = down_rows(inner_ref[0:1, :] / D)

    for sub in range(x_ref.shape[1] // LANES):
        at = lanes_of(sub)
        gradient = input_gradient(gn_ref, x_ref, at, scale, mean)
        top_ref[:, at] = gradient[:half]
        bottom_ref[:, at] = gradient[half:]


def fold_kernel(odd_ref, first_ref, second_ref, *rest):
    out_ref = rest[-1]
    half = first_ref.shape[0]
    odd = odd_ref[0]

    @pl.when(odd == 0)
    def _():
        out_ref[:half] = first_ref[...]
        out_ref[half:] = second_ref[...]

    @pl.when(odd != 0)
    def _():
        out_ref[:half] = second_ref[...]
        out_ref[half:] = first_ref[...]


def taps_kernel(seqs, *refs):
    per = 3
    ins, (out_ref, flipped) = refs[: per * seqs], refs[-2:]
    rows = ins[0].shape[0]
    half = rows // 2
    count = LANES // GROUP
    step = pl.program_id(0)

    owner = lax.broadcasted_iota(jnp.int32, (half, LANES), 1) // GROUP
    row = lax.broadcasted_iota(jnp.int32, (half, LANES), 0)
    col = lax.broadcasted_iota(jnp.int32, (half, LANES), 1)
    masks = [(owner == g).astype(bf16) for g in range(count)]
    blocks = ins[0].shape[1] // LANES
    found = []
    for sub in range(blocks):
        at = lanes_of(sub)
        grads = []
        signals = []
        for s in range(seqs):
            gz_ref, own_ref, halo_ref = ins[per * s : per * s + 3]
            grads += [gz_ref[:half, at], gz_ref[half:, at]]
            signal = jnp.concatenate([halo_ref[:, at], own_ref[:, at]], axis=0)
            signals.append(windows(signal, half))
        wide = jnp.concatenate(grads, axis=1)
        left = jnp.concatenate(
            [wide * jnp.concatenate([masks[g]] * len(grads), axis=1) for g in range(count)],
            axis=0,
        )
        products = lax.dot_general(
            left,
            jnp.concatenate(signals, axis=1),
            (((1,), (1,)), ((), ())),
            preferred_element_type=f32,
        )
        slabs = []
        for g in range(count):
            mine = products[g * half : (g + 1) * half]
            wheel = jnp.where(col > row, mine[:, :LANES], mine[:, LANES:])
            slab = wheel[:SUB]
            for a in range(SUB, half, SUB):
                slab = slab + pltpu.roll(wheel[a : a + SUB], LANES - a, 1)
            slabs.append(slab)
        slabs = jnp.concatenate(slabs, axis=0)
        within = lax.rem(lax.broadcasted_iota(jnp.int32, slabs.shape, 0), SUB)
        for bit in (1, 2, 4):
            turned = pltpu.roll(slabs, LANES - bit, 1)
            slabs = jnp.where(within & bit != 0, turned, slabs)
        found.append(jnp.sum(slabs.reshape(count, SUB, LANES), axis=1))
    here = blocks * count
    flipped[pl.ds(pl.multiple_of(step * here, here), here), :] = jnp.concatenate(found, axis=0)

    @pl.when(step == pl.num_programs(0) - 1)
    def _():
        out_ref[...] = lax.dot_general(
            lag_flip(out_ref.shape[0]),
            flipped[...].astype(bf16),
            (((1,), (1,)), ((), ())),
            preferred_element_type=f32,
        )


class Calls:
    def __init__(self, rows, width, taps):
        self.rows, self.width, self.taps = rows, width, taps
        self.block = min(BLOCK, width)
        self.steps = width // self.block
        self.latest = None

    def flat(self, array, s=None, layer=None, rows=None):
        rows = self.rows if rows is None else rows
        lead = tuple(i for i in (layer, s) if i is not None)
        spec = pl.BlockSpec(
            (None,) * len(lead) + (rows, self.block), lambda j, *_: lead + (0, j)
        )
        return array, spec

    def small(self, array=None, s=0):
        return array, pl.BlockSpec((SUB, self.rows), lambda j, *_: (s, 0))

    def filters(self, array, layer):
        count = self.block // GROUP
        return array, pl.BlockSpec((None, count, self.taps), lambda j, *_: (layer, j, 0))

    def square(self):
        return pltpu.VMEM((self.rows, self.rows), f32)

    def call(self, kernel, name, ins, outs, scratch=(), carry=None, prefetch=()):
        operands = [a for a, _ in ins]
        in_specs = [b for _, b in ins]
        aliases = {}
        if self.latest is not None and self.latest is not carry:
            operands.append(self.latest)
            in_specs.append(pl.BlockSpec(memory_space=pl.ANY))
        if carry is not None:
            aliases = {len(prefetch) + len(operands): 0}
            operands.append(carry)
            in_specs.append(pl.BlockSpec(memory_space=pl.ANY))
        results = pl.pallas_call(
            kernel,
            name=name,
            out_shape=[jax.ShapeDtypeStruct(s, d) for s, d, _ in outs],
            grid_spec=pltpu.PrefetchScalarGridSpec(
                num_scalar_prefetch=len(prefetch),
                grid=(self.steps,),
                in_specs=in_specs,
                out_specs=[b for _, _, b in outs],
                scratch_shapes=list(scratch),
            ),
            input_output_aliases=aliases,
            compiler_params=pltpu.CompilerParams(
                dimension_semantics=("arbitrary",), vmem_limit_bytes=VMEM_LIMIT
            ),
            cost_estimate=pl.CostEstimate(
                flops=1, bytes_accessed=1, transcendentals=0
            ),
        )(*prefetch, *operands)
        self.latest = results[-1]
        return results


def shifted(value, steps):
    count = lax.axis_size("ctx")
    first, last = max(0, -steps), min(count, count - steps)
    return lax.ppermute(value, "ctx", [(r, r + steps) for r in range(first, last)])


def over_channels(value):
    if lax.axis_size("ch") == 2:
        return value + lax.ppermute(value, "ch", [(0, 1), (1, 0)])
    return lax.psum(value, "ch")


def owner_routes(count):
    blocks = [[], []]
    for block in range(2 * count):
        folded = block if block < count else 2 * count - 1 - block
        blocks[block % 2].append((folded, block // 2))
    return blocks


def local(activations, grad_in, gate_out, gate_in, filters):
    seqs, rows, width = activations.shape
    taps = filters.shape[2]
    assert rows == taps == LANES
    half = rows // 2
    last = LAYERS - 1
    c = Calls(rows, width, taps)
    one = ((rows, width), bf16, c.flat(None)[1])
    part = ((half, width), bf16, c.flat(None, rows=half)[1])
    vector = ((SUB, rows), f32, c.small()[1])
    whole = (gate_out.shape, bf16)
    routes = owner_routes(lax.axis_size("ctx"))
    odd = lax.rem(lax.axis_index("ctx"), 2)

    def table():
        return [[None] * seqs for _ in range(LAYERS)]

    x, z, u, u_halo, tot = table(), table(), table(), table(), table()
    gz, gz_halo, gn, inner = table(), table(), table(), table()
    done = {"out": None, "in": None, "fold": None}
    found = [None] * LAYERS
    returned = [[None, None] for _ in range(seqs)]
    arrived = [None, None]

    def squares():
        (ssq,) = c.call(
            squares_kernel, "squares",
            [(activations, pl.BlockSpec((seqs, rows, c.block), lambda j: (0, 0, j)))],
            [((seqs * SUB, rows), f32, pl.BlockSpec((seqs * SUB, rows), lambda j: (0, 0)))],
            [pltpu.VMEM((seqs, rows, rows), f32)],
        )
        total = over_channels(ssq)
        for s in range(seqs):
            x[0][s] = c.flat(activations, s)
            tot[0][s] = c.small(total, s)

    def gated_input(layer, s):
        (u[layer][s],) = c.call(
            input_kernel, "input",
            [x[layer][s], tot[layer][s], c.flat(gate_in, s, layer)], [one], [c.square()],
        )
        u_halo[layer][s] = shifted(u[layer][s], 1)

    def arrive():
        held, _ = lax.optimization_barrier((grad_in, c.latest))
        for side in range(2):
            start = jnp.where(odd == side, 0, half)
            piece = lax.dynamic_slice_in_dim(held, start, half, axis=1)
            arrived[side] = lax.ppermute(piece, "ctx", routes[side])

    def arrived_of(s):
        return [c.flat(arrived[side], s, rows=half) for side in range(2)]

    def forward(layer, s):
        z[layer][s], nx, ssq = c.call(
            forward_kernel, "forward",
            [c.filters(filters, layer), c.flat(u[layer][s]), c.flat(u_halo[layer][s]),
             c.flat(gate_out, s, layer)],
            [one, one, vector], [c.square()],
        )
        x[layer + 1][s] = c.flat(nx)
        tot[layer + 1][s] = c.small(over_channels(ssq))

    def last_forward(s):
        (done["out"],) = c.call(
            last_forward_kernel, "last_forward",
            [c.filters(filters, last), c.flat(u[last][s]), c.flat(u_halo[last][s])]
            + arrived_of(s),
            [whole + (c.flat(None, s, last)[1],)], carry=done["out"],
        )

    def first_gate(s):
        (gz[last][s],) = c.call(
            gate_kernel, "gate", arrived_of(s) + [c.flat(gate_out, s, last)], [one]
        )
        gz_halo[last][s] = shifted(gz[last][s], -1)

    def backward(layer, s):
        done["in"], gn[layer][s], found_inner = c.call(
            backward_kernel, "backward",
            [c.filters(filters, layer), c.flat(gz[layer][s]), c.flat(gz_halo[layer][s]),
             tot[layer][s], x[layer][s], c.flat(gate_in, s, layer)],
            [whole + (c.flat(None, s, layer)[1],), one, vector],
            [c.square()] * 2, carry=done["in"],
        )
        inner[layer][s] = c.small(over_channels(found_inner))

    def common(layer, s):
        return [c.flat(gn[layer][s]), x[layer][s], tot[layer][s], inner[layer][s]]

    def between(layer, s):
        done["out"], gz[layer - 1][s] = c.call(
            between_kernel, "between",
            common(layer, s) + [c.flat(z[layer - 1][s]), c.flat(gate_out, s, layer - 1)],
            [whole + (c.flat(None, s, layer - 1)[1],), one],
            [c.square()] * 2, carry=done["out"],
        )
        gz_halo[layer - 1][s] = shifted(gz[layer - 1][s], -1)

    def finish(s):
        halves = c.call(
            finish_kernel, "finish", common(0, s), [part, part], [c.square()] * 2
        )
        for side in range(2):
            back = [(d, r) for r, d in routes[side]]
            returned[s][side] = lax.ppermute(halves[side], "ctx", back)

    def taps_of(layer):
        ins = []
        for s in range(seqs):
            ins += [c.flat(gz[layer][s]), c.flat(u[layer][s]), c.flat(u_halo[layer][s])]
        groups = width // GROUP
        (found[layer],) = c.call(
            functools.partial(taps_kernel, seqs), "taps", ins,
            [((taps, groups), f32, pl.BlockSpec((taps, groups), lambda j: (0, 0)))],
            [pltpu.VMEM((groups, taps), f32)],
        )

    def fold(s):
        (done["fold"],) = c.call(
            fold_kernel, "fold",
            [c.flat(returned[s][side], rows=half) for side in range(2)],
            [(activations.shape, bf16, c.flat(None, s)[1])],
            carry=done["fold"], prefetch=(odd.reshape(1).astype(jnp.int32),),
        )

    squares()
    for s in range(seqs):
        gated_input(0, s)
    arrive()
    for s in range(seqs):
        forward(0, s)
        gated_input(1, s)
    for s in range(seqs):
        first_gate(s)
    for layer in range(1, last):
        for s in range(seqs):
            forward(layer, s)
            gated_input(layer + 1, s)
    for s in range(seqs):
        backward(last, s)
    for s in range(seqs):
        between(last, s)
    for s in range(seqs):
        last_forward(s)
    for layer in reversed(range(1, last)):
        for s in range(seqs):
            backward(layer, s)
            between(layer, s)
        taps_of(layer + 1)
    for s in range(seqs):
        backward(0, s)
        finish(s)
    for layer in reversed(range(min(2, LAYERS))):
        taps_of(layer)

    count = lax.axis_size("ctx")
    mine = lax.all_to_all(jnp.stack(found), "ctx", split_axis=1, concat_axis=1, tiled=True)
    mine = jnp.sum(mine.reshape(LAYERS, count, taps // count, width // GROUP), axis=1)
    grad_filters = jnp.swapaxes(mine, 1, 2)
    for s in range(seqs):
        fold(s)
    return done["fold"], done["out"], done["in"], grad_filters


def solution(mesh):
    return jax.shard_map(
        local,
        mesh=mesh,
        in_specs=(
            P(None, "ctx", "ch"),
            P(None, "ctx", "ch"),
            P(None, None, "ctx", "ch"),
            P(None, None, "ctx", "ch"),
            P(None, "ch", None),
        ),
        out_specs=(
            P(None, "ctx", "ch"),
            P(None, None, "ctx", "ch"),
            P(None, None, "ctx", "ch"),
            P(None, "ch", "ctx"),
        ),
        check_vma=False,
    )
```

```python
import functools

import jax
import jax.numpy as jnp
from jax import lax
from jax.experimental import pallas as pl
from jax.experimental.pallas import tpu as pltpu
from jax.sharding import PartitionSpec as P

D = 8192
GROUP = 16
LAYERS = 3
EPS = 1e-06
LANES = 128
SUB = 8
BLOCK = 1024
HEIGHT = 32
VMEM_LIMIT = 28 * 1024 * 1024
VMEM_MOST = 60 * 1024 * 1024

f32 = jnp.float32
bf16 = jnp.bfloat16


def down_rows(row):
    count = row.shape[1]
    return jnp.broadcast_to(row, (count, count)).T


def lane_sums(acc):
    return jnp.broadcast_to(jnp.sum(acc.T, axis=0, keepdims=True), (SUB, acc.shape[0]))


def lag_flip(taps):
    row = lax.broadcasted_iota(jnp.int32, (taps, taps), 0)
    col = lax.broadcasted_iota(jnp.int32, (taps, taps), 1)
    return (lax.rem(row + col, taps) == 0).astype(bf16)


def band_masks(height, taps, behind):
    row = lax.broadcasted_iota(jnp.int32, (height, taps), 0)
    col = lax.broadcasted_iota(jnp.int32, (height, taps), 1)
    first = (col > row) if behind else (col >= row)
    return jnp.concatenate(
        [jnp.where(first, 1.0, 0.0), jnp.where(first, 0.0, 1.0)], axis=1
    ).astype(bf16)


def band(taps_row, masks):
    height, taps = masks.shape[0], taps_row.shape[1]
    wheel = pltpu.roll(
        jnp.broadcast_to(taps_row, (height, taps)), 0, 1, stride=1, stride_axis=0
    ).astype(bf16)
    return jnp.concatenate([wheel, wheel], axis=1) * masks


def windows(signal, height):
    count = signal.shape[0] // 2 // height
    return jnp.concatenate(
        [signal]
        + [
            jnp.concatenate([signal[k * height :], signal[: k * height]], axis=0)
            for k in range(1, count)
        ],
        axis=1,
    )


def group_pick(stacked, height, sides):
    count = LANES // GROUP
    owner = lax.broadcasted_iota(jnp.int32, (height, LANES), 1) // GROUP
    parts = []
    for side in range(sides):
        at = lanes_of(side)
        picked = stacked[:height, at]
        for g in range(1, count):
            picked = jnp.where(owner == g, stacked[g * height : (g + 1) * height, at], picked)
        parts.append(picked)
    return jnp.concatenate(parts, axis=0)


def filtered_block(taps_rows, signal, masks):
    height = masks.shape[0]
    count = LANES // GROUP
    bands = jnp.concatenate([band(taps_rows[g : g + 1], masks) for g in range(count)], axis=0)
    stacked = jnp.dot(bands, windows(signal, height), preferred_element_type=f32)
    return group_pick(stacked, height, signal.shape[0] // 2 // height)


def lanes_of(index):
    return slice(index * LANES, (index + 1) * LANES)


def groups_of(index):
    count = LANES // GROUP
    return slice(index * count, (index + 1) * count)


def scale_of(total_ref):
    return down_rows(lax.rsqrt(total_ref[0:1, :] / D + EPS))


def squares_kernel(x_ref, ssq_ref, acc_ref):
    step = pl.program_id(0)

    @pl.when(step == 0)
    def _():
        acc_ref[...] = jnp.zeros_like(acc_ref)

    for s in range(x_ref.shape[0]):
        for sub in range(x_ref.shape[2] // LANES):
            values = x_ref[s, :, lanes_of(sub)].astype(f32)
            acc_ref[s] += values * values

    @pl.when(step == pl.num_programs(0) - 1)
    def _():
        for s in range(x_ref.shape[0]):
            ssq_ref[s * SUB : (s + 1) * SUB] = lane_sums(acc_ref[s])


def input_kernel(x_ref, tot_ref, gate_ref, *rest):
    u_ref, scale = rest[-2:]

    @pl.when(pl.program_id(0) == 0)
    def _():
        scale[...] = scale_of(tot_ref)

    for sub in range(x_ref.shape[1] // LANES):
        at = lanes_of(sub)
        normed = x_ref[:, at].astype(f32) * scale[...]
        u_ref[:, at] = (gate_ref[:, at].astype(f32) * normed).astype(bf16)


def behind_block(taps, own_ref, halo_ref, sub, masks):
    at = lanes_of(sub)
    signal = jnp.concatenate([halo_ref[:, at], own_ref[:, at]], axis=0)
    return filtered_block(taps[groups_of(sub)], signal, masks)


def flipped_taps(taps_ref):
    return jnp.dot(taps_ref[...], lag_flip(taps_ref.shape[1]), preferred_element_type=f32)


def forward_kernel(taps_ref, own_ref, halo_ref, gate_ref, *rest):
    z_ref, x_ref, ssq_ref, acc_ref = rest[-4:]
    step = pl.program_id(0)

    @pl.when(step == 0)
    def _():
        acc_ref[...] = jnp.zeros_like(acc_ref)

    taps = flipped_taps(taps_ref)
    masks = band_masks(HEIGHT, taps.shape[1], True)
    for sub in range(own_ref.shape[1] // LANES):
        at = lanes_of(sub)
        z = behind_block(taps, own_ref, halo_ref, sub, masks)
        z_ref[:, at] = z.astype(bf16)
        x = (gate_ref[:, at].astype(f32) * z).astype(bf16)
        x_ref[:, at] = x
        values = x.astype(f32)
        acc_ref[...] += values * values

    @pl.when(step == pl.num_programs(0) - 1)
    def _():
        ssq_ref[...] = lane_sums(acc_ref[...])


def last_forward_kernel(taps_ref, own_ref, halo_ref, top_ref, bottom_ref, *rest):
    out_ref = rest[-1]
    taps = flipped_taps(taps_ref)
    masks = band_masks(HEIGHT, taps.shape[1], True)
    for sub in range(own_ref.shape[1] // LANES):
        at = lanes_of(sub)
        z = behind_block(taps, own_ref, halo_ref, sub, masks)
        gradient = jnp.concatenate([top_ref[:, at], bottom_ref[:, at]], axis=0).astype(f32)
        out_ref[:, at] = (gradient * z).astype(bf16)


def gate_kernel(top_ref, bottom_ref, gate_ref, *rest):
    gz_ref = rest[-1]
    half = top_ref.shape[0]
    gz_ref[:half] = (top_ref[...].astype(f32) * gate_ref[:half].astype(f32)).astype(bf16)
    gz_ref[half:] = (bottom_ref[...].astype(f32) * gate_ref[half:].astype(f32)).astype(bf16)


def backward_kernel(taps_ref, own_ref, halo_ref, tot_ref, x_ref, gate_ref, *rest):
    out_ref, gn_ref, inner_ref, scale, acc_ref = rest[-5:]
    step = pl.program_id(0)

    @pl.when(step == 0)
    def _():
        scale[...] = scale_of(tot_ref)
        acc_ref[...] = jnp.zeros_like(acc_ref)

    taps = taps_ref[...].astype(f32)
    masks = band_masks(HEIGHT, taps.shape[1], False)
    for sub in range(own_ref.shape[1] // LANES):
        at = lanes_of(sub)
        signal = jnp.concatenate([own_ref[:, at], halo_ref[:, at]], axis=0)
        gu = filtered_block(taps[groups_of(sub)], signal, masks)
        normed = x_ref[:, at].astype(f32) * scale[...]
        out_ref[:, at] = (gu * normed).astype(bf16)
        gn = gu * gate_ref[:, at].astype(f32)
        gn_ref[:, at] = gn.astype(bf16)
        acc_ref[...] += gn * normed

    @pl.when(step == pl.num_programs(0) - 1)
    def _():
        inner_ref[...] = lane_sums(acc_ref[...])


def input_gradient(gn_ref, x_ref, at, scale, mean):
    normed = x_ref[:, at].astype(f32) * scale[...]
    return (scale[...] * (gn_ref[:, at].astype(f32) - normed * mean[...])).astype(bf16)


def between_kernel(gn_ref, x_ref, tot_ref, inner_ref, z_ref, gate_ref, *rest):
    out_ref, gz_ref, scale, mean = rest[-4:]

    @pl.when(pl.program_id(0) == 0)
    def _():
        scale[...] = scale_of(tot_ref)
        mean[...] = down_rows(inner_ref[0:1, :] / D)

    for sub in range(x_ref.shape[1] // LANES):
        at = lanes_of(sub)
        gradient = input_gradient(gn_ref, x_ref, at, scale, mean).astype(f32)
        gz_ref[:, at] = (gate_ref[:, at].astype(f32) * gradient).astype(bf16)
        out_ref[:, at] = (gradient * z_ref[:, at].astype(f32)).astype(bf16)


def finish_kernel(gn_ref, x_ref, tot_ref, inner_ref, *rest):
    top_ref, bottom_ref, scale, mean = rest[-4:]
    half = top_ref.shape[0]

    @pl.when(pl.program_id(0) == 0)
    def _():
        scale[...] = scale_of(tot_ref)
        mean[...] = down_rows(inner_ref[0:1, :] / D)

    for sub in range(x_ref.shape[1] // LANES):
        at = lanes_of(sub)
        gradient = input_gradient(gn_ref, x_ref, at, scale, mean)
        top_ref[:, at] = gradient[:half]
        bottom_ref[:, at] = gradient[half:]


def fold_kernel(odd_ref, first_ref, second_ref, *rest):
    out_ref = rest[-1]
    half = first_ref.shape[0]
    odd = odd_ref[0]

    @pl.when(odd == 0)
    def _():
        out_ref[:half] = first_ref[...]
        out_ref[half:] = second_ref[...]

    @pl.when(odd != 0)
    def _():
        out_ref[:half] = second_ref[...]
        out_ref[half:] = first_ref[...]


def taps_kernel(seqs, *refs):
    per = 3
    ins, (out_ref, flipped) = refs[: per * seqs], refs[-2:]
    rows = ins[0].shape[0]
    half = rows // 2
    count = LANES // GROUP
    step = pl.program_id(0)

    owner = lax.broadcasted_iota(jnp.int32, (half, LANES), 1) // GROUP
    row = lax.broadcasted_iota(jnp.int32, (half, LANES), 0)
    col = lax.broadcasted_iota(jnp.int32, (half, LANES), 1)
    masks = [(owner == g).astype(bf16) for g in range(count)]
    blocks = ins[0].shape[1] // LANES
    found = []
    for sub in range(blocks):
        at = lanes_of(sub)
        grads = []
        signals = []
        for s in range(seqs):
            gz_ref, own_ref, halo_ref = ins[per * s : per * s + 3]
            grads += [gz_ref[:half, at], gz_ref[half:, at]]
            signal = jnp.concatenate([halo_ref[:, at], own_ref[:, at]], axis=0)
            signals.append(windows(signal, half))
        wide = jnp.concatenate(grads, axis=1)
        left = jnp.concatenate(
            [wide * jnp.concatenate([masks[g]] * len(grads), axis=1) for g in range(count)],
            axis=0,
        )
        products = lax.dot_general(
            left,
            jnp.concatenate(signals, axis=1),
            (((1,), (1,)), ((), ())),
            preferred_element_type=f32,
        )
        slabs = []
        for g in range(count):
            mine = products[g * half : (g + 1) * half]
            wheel = jnp.where(col > row, mine[:, :LANES], mine[:, LANES:])
            slab = wheel[:SUB]
            for a in range(SUB, half, SUB):
                slab = slab + pltpu.roll(wheel[a : a + SUB], LANES - a, 1)
            slabs.append(slab)
        slabs = jnp.concatenate(slabs, axis=0)
        within = lax.rem(lax.broadcasted_iota(jnp.int32, slabs.shape, 0), SUB)
        for bit in (1, 2, 4):
            turned = pltpu.roll(slabs, LANES - bit, 1)
            slabs = jnp.where(within & bit != 0, turned, slabs)
        found.append(jnp.sum(slabs.reshape(count, SUB, LANES), axis=1))
    here = blocks * count
    flipped[pl.ds(pl.multiple_of(step * here, here), here), :] = jnp.concatenate(found, axis=0)

    @pl.when(step == pl.num_programs(0) - 1)
    def _():
        out_ref[...] = lax.dot_general(
            lag_flip(out_ref.shape[0]),
            flipped[...].astype(bf16),
            (((1,), (1,)), ((), ())),
            preferred_element_type=f32,
        )


def pack_kernel(*refs):
    out_ref = refs[-1]
    for layer in range(LAYERS):
        out_ref[layer] = refs[layer][...]


class Calls:
    def __init__(self, rows, width, taps):
        self.rows, self.width, self.taps = rows, width, taps
        self.block = min(BLOCK, width)
        self.steps = width // self.block
        self.latest = None

    def flat(self, array, s=None, layer=None, rows=None):
        rows = self.rows if rows is None else rows
        lead = tuple(i for i in (layer, s) if i is not None)
        spec = pl.BlockSpec(
            (None,) * len(lead) + (rows, self.block), lambda j, *_: lead + (0, j)
        )
        return array, spec

    def small(self, array=None, s=0):
        return array, pl.BlockSpec((SUB, self.rows), lambda j, *_: (s, 0))

    def filters(self, array, layer):
        count = self.block // GROUP
        return array, pl.BlockSpec((None, count, self.taps), lambda j, *_: (layer, j, 0))

    def square(self):
        return pltpu.VMEM((self.rows, self.rows), f32)

    def call(self, kernel, name, ins, outs, scratch=(), carry=None, prefetch=(), vmem=VMEM_LIMIT):
        operands = [a for a, _ in ins]
        in_specs = [b for _, b in ins]
        aliases = {}
        if self.latest is not None and self.latest is not carry:
            operands.append(self.latest)
            in_specs.append(pl.BlockSpec(memory_space=pl.ANY))
        if carry is not None:
            aliases = {len(prefetch) + len(operands): 0}
            operands.append(carry)
            in_specs.append(pl.BlockSpec(memory_space=pl.ANY))
        results = pl.pallas_call(
            kernel,
            name=name,
            out_shape=[jax.ShapeDtypeStruct(s, d) for s, d, _ in outs],
            grid_spec=pltpu.PrefetchScalarGridSpec(
                num_scalar_prefetch=len(prefetch),
                grid=(self.steps,),
                in_specs=in_specs,
                out_specs=[b for _, _, b in outs],
                scratch_shapes=list(scratch),
            ),
            input_output_aliases=aliases,
            compiler_params=pltpu.CompilerParams(
                dimension_semantics=("arbitrary",), vmem_limit_bytes=vmem
            ),
            cost_estimate=pl.CostEstimate(
                flops=1, bytes_accessed=1, transcendentals=0
            ),
        )(*prefetch, *operands)
        self.latest = results[-1]
        return results


def shifted(value, steps):
    count = lax.axis_size("ctx")
    first, last = max(0, -steps), min(count, count - steps)
    return lax.ppermute(value, "ctx", [(r, r + steps) for r in range(first, last)])


def over_channels(value):
    if lax.axis_size("ch") == 2:
        return value + lax.ppermute(value, "ch", [(0, 1), (1, 0)])
    return lax.psum(value, "ch")


def owner_routes(count):
    blocks = [[], []]
    for block in range(2 * count):
        folded = block if block < count else 2 * count - 1 - block
        blocks[block % 2].append((folded, block // 2))
    return blocks


def local(activations, grad_in, gate_out, gate_in, filters):
    seqs, rows, width = activations.shape
    taps = filters.shape[2]
    assert rows == taps == LANES
    half = rows // 2
    last = LAYERS - 1
    c = Calls(rows, width, taps)
    one = ((rows, width), bf16, c.flat(None)[1])
    part = ((half, width), bf16, c.flat(None, rows=half)[1])
    vector = ((SUB, rows), f32, c.small()[1])
    whole = (gate_out.shape, bf16)
    routes = owner_routes(lax.axis_size("ctx"))
    odd = lax.rem(lax.axis_index("ctx"), 2)

    def table():
        return [[None] * seqs for _ in range(LAYERS)]

    x, z, u, u_halo, tot = table(), table(), table(), table(), table()
    gz, gz_halo, gn, inner = table(), table(), table(), table()
    done = {"out": None, "in": None, "fold": None}
    found = [None] * LAYERS
    returned = [[None, None] for _ in range(seqs)]
    arrived = [None, None]

    def squares():
        (ssq,) = c.call(
            squares_kernel, "squares",
            [(activations, pl.BlockSpec((seqs, rows, c.block), lambda j: (0, 0, j)))],
            [((seqs * SUB, rows), f32, pl.BlockSpec((seqs * SUB, rows), lambda j: (0, 0)))],
            [pltpu.VMEM((seqs, rows, rows), f32)], vmem=VMEM_MOST,
        )
        total = over_channels(ssq)
        for s in range(seqs):
            x[0][s] = c.flat(activations, s)
            tot[0][s] = c.small(total, s)

    def gated_input(layer, s):
        (u[layer][s],) = c.call(
            input_kernel, "input",
            [x[layer][s], tot[layer][s], c.flat(gate_in, s, layer)], [one], [c.square()],
            vmem=VMEM_LIMIT if layer else VMEM_MOST,
        )
        u_halo[layer][s] = shifted(u[layer][s], 1)

    def arrive():
        for side in range(2):
            start = jnp.where(odd == side, 0, half)
            piece = lax.dynamic_slice_in_dim(grad_in, start, half, axis=1)
            arrived[side] = lax.ppermute(piece, "ctx", routes[side])

    def arrived_of(s):
        return [c.flat(arrived[side], s, rows=half) for side in range(2)]

    def forward(layer, s):
        z[layer][s], nx, ssq = c.call(
            forward_kernel, "forward",
            [c.filters(filters, layer), c.flat(u[layer][s]), c.flat(u_halo[layer][s]),
             c.flat(gate_out, s, layer)],
            [one, one, vector], [c.square()],
        )
        x[layer + 1][s] = c.flat(nx)
        tot[layer + 1][s] = c.small(over_channels(ssq))

    def last_forward(s):
        (done["out"],) = c.call(
            last_forward_kernel, "last_forward",
            [c.filters(filters, last), c.flat(u[last][s]), c.flat(u_halo[last][s])]
            + arrived_of(s),
            [whole + (c.flat(None, s, last)[1],)], carry=done["out"],
        )

    def first_gate(s):
        (gz[last][s],) = c.call(
            gate_kernel, "gate", arrived_of(s) + [c.flat(gate_out, s, last)], [one]
        )
        gz_halo[last][s] = shifted(gz[last][s], -1)

    def backward(layer, s):
        done["in"], gn[layer][s], found_inner = c.call(
            backward_kernel, "backward",
            [c.filters(filters, layer), c.flat(gz[layer][s]), c.flat(gz_halo[layer][s]),
             tot[layer][s], x[layer][s], c.flat(gate_in, s, layer)],
            [whole + (c.flat(None, s, layer)[1],), one, vector],
            [c.square()] * 2, carry=done["in"],
        )
        inner[layer][s] = c.small(over_channels(found_inner))

    def common(layer, s):
        return [c.flat(gn[layer][s]), x[layer][s], tot[layer][s], inner[layer][s]]

    def between(layer, s):
        done["out"], gz[layer - 1][s] = c.call(
            between_kernel, "between",
            common(layer, s) + [c.flat(z[layer - 1][s]), c.flat(gate_out, s, layer - 1)],
            [whole + (c.flat(None, s, layer - 1)[1],), one],
            [c.square()] * 2, carry=done["out"],
        )
        gz_halo[layer - 1][s] = shifted(gz[layer - 1][s], -1)

    def finish(s):
        halves = c.call(
            finish_kernel, "finish", common(0, s), [part, part], [c.square()] * 2
        )
        for side in range(2):
            back = [(d, r) for r, d in routes[side]]
            returned[s][side] = lax.ppermute(halves[side], "ctx", back)

    def taps_of(layer):
        ins = []
        for s in range(seqs):
            ins += [c.flat(gz[layer][s]), c.flat(u[layer][s]), c.flat(u_halo[layer][s])]
        groups = width // GROUP
        (found[layer],) = c.call(
            functools.partial(taps_kernel, seqs), "taps", ins,
            [((taps, groups), f32, pl.BlockSpec((taps, groups), lambda j: (0, 0)))],
            [pltpu.VMEM((groups, taps), f32)],
        )

    def fold(s):
        (done["fold"],) = c.call(
            fold_kernel, "fold",
            [c.flat(returned[s][side], rows=half) for side in range(2)],
            [(activations.shape, bf16, c.flat(None, s)[1])],
            carry=done["fold"], prefetch=(odd.reshape(1).astype(jnp.int32),),
        )

    def pack():
        groups = width // GROUP
        shape = (LAYERS, taps, groups)
        spec = pl.BlockSpec((taps, groups), lambda: (0, 0))
        return pl.pallas_call(
            pack_kernel,
            name="pack",
            out_shape=jax.ShapeDtypeStruct(shape, f32),
            in_specs=[spec] * LAYERS + [pl.BlockSpec(memory_space=pl.ANY)],
            out_specs=pl.BlockSpec(shape, lambda: (0, 0, 0)),
        )(*found, returned[0][0])

    arrive()
    squares()
    for s in range(seqs):
        gated_input(0, s)
    for s in range(seqs):
        forward(0, s)
        gated_input(1, s)
    for s in range(seqs):
        first_gate(s)
    for layer in range(1, last):
        for s in range(seqs):
            forward(layer, s)
            gated_input(layer + 1, s)
    for s in range(seqs):
        backward(last, s)
        between(last, s)
    for s in range(seqs):
        last_forward(s)
    for layer in reversed(range(1, last)):
        for s in range(seqs):
            backward(layer, s)
            between(layer, s)
    for layer in reversed(range(LAYERS)):
        taps_of(layer)
    for s in range(seqs):
        backward(0, s)
        finish(s)

    count = lax.axis_size("ctx")
    mine = lax.all_to_all(pack(), "ctx", split_axis=1, concat_axis=1, tiled=True)
    mine = jnp.sum(mine.reshape(LAYERS, count, taps // count, width // GROUP), axis=1)
    grad_filters = jnp.swapaxes(mine, 1, 2)
    for s in range(seqs):
        fold(s)
    return done["fold"], done["out"], done["in"], grad_filters


def solution(mesh):
    return jax.shard_map(
        local,
        mesh=mesh,
        in_specs=(
            P(None, "ctx", "ch"),
            P(None, "ctx", "ch"),
            P(None, None, "ctx", "ch"),
            P(None, None, "ctx", "ch"),
            P(None, "ch", None),
        ),
        out_specs=(
            P(None, "ctx", "ch"),
            P(None, None, "ctx", "ch"),
            P(None, None, "ctx", "ch"),
            P(None, "ch", "ctx"),
        ),
        check_vma=False,
    )
```

```python
import functools

import jax
import jax.numpy as jnp
from jax import lax
from jax.experimental import pallas as pl
from jax.experimental.pallas import tpu as pltpu
from jax.sharding import PartitionSpec as P

D = 8192
GROUP = 16
LAYERS = 3
EPS = 1e-06
LANES = 128
SUB = 8
BLOCK = 1024
HEIGHT = 32
VMEM_LIMIT = 28 * 1024 * 1024
VMEM_MOST = 60 * 1024 * 1024

f32 = jnp.float32
bf16 = jnp.bfloat16


def down_rows(row):
    count = row.shape[1]
    return jnp.broadcast_to(row, (count, count)).T


def lane_sums(acc):
    return jnp.broadcast_to(jnp.sum(acc.T, axis=0, keepdims=True), (SUB, acc.shape[0]))


def lag_flip(taps):
    row = lax.broadcasted_iota(jnp.int32, (taps, taps), 0)
    col = lax.broadcasted_iota(jnp.int32, (taps, taps), 1)
    return (lax.rem(row + col, taps) == 0).astype(bf16)


def band_masks(height, taps, behind):
    row = lax.broadcasted_iota(jnp.int32, (height, taps), 0)
    col = lax.broadcasted_iota(jnp.int32, (height, taps), 1)
    first = (col > row) if behind else (col >= row)
    return jnp.concatenate(
        [jnp.where(first, 1.0, 0.0), jnp.where(first, 0.0, 1.0)], axis=1
    ).astype(bf16)


def band(taps_row, masks):
    height, taps = masks.shape[0], taps_row.shape[1]
    wheel = pltpu.roll(
        jnp.broadcast_to(taps_row, (height, taps)), 0, 1, stride=1, stride_axis=0
    ).astype(bf16)
    return jnp.concatenate([wheel, wheel], axis=1) * masks


def windows(signal, height):
    count = signal.shape[0] // 2 // height
    return jnp.concatenate(
        [signal]
        + [
            jnp.concatenate([signal[k * height :], signal[: k * height]], axis=0)
            for k in range(1, count)
        ],
        axis=1,
    )


def group_pick(stacked, height, sides):
    count = LANES // GROUP
    owner = lax.broadcasted_iota(jnp.int32, (height, LANES), 1) // GROUP
    parts = []
    for side in range(sides):
        at = lanes_of(side)
        picked = stacked[:height, at]
        for g in range(1, count):
            picked = jnp.where(owner == g, stacked[g * height : (g + 1) * height, at], picked)
        parts.append(picked)
    return jnp.concatenate(parts, axis=0)


def filtered_block(taps_rows, signal, masks):
    height = masks.shape[0]
    count = LANES // GROUP
    bands = jnp.concatenate([band(taps_rows[g : g + 1], masks) for g in range(count)], axis=0)
    stacked = jnp.dot(bands, windows(signal, height), preferred_element_type=f32)
    return group_pick(stacked, height, signal.shape[0] // 2 // height)


def lanes_of(index):
    return slice(index * LANES, (index + 1) * LANES)


def groups_of(index):
    count = LANES // GROUP
    return slice(index * count, (index + 1) * count)


def scale_of(total_ref):
    return down_rows(lax.rsqrt(total_ref[0:1, :] / D + EPS))


def squares_kernel(x_ref, ssq_ref, acc_ref):
    step = pl.program_id(0)

    @pl.when(step == 0)
    def _():
        acc_ref[...] = jnp.zeros_like(acc_ref)

    for s in range(x_ref.shape[0]):
        for sub in range(x_ref.shape[2] // LANES):
            values = x_ref[s, :, lanes_of(sub)].astype(f32)
            acc_ref[s] += values * values

    @pl.when(step == pl.num_programs(0) - 1)
    def _():
        for s in range(x_ref.shape[0]):
            ssq_ref[s * SUB : (s + 1) * SUB] = lane_sums(acc_ref[s])


def input_kernel(x_ref, tot_ref, gate_ref, *rest):
    u_ref, scale = rest[-2:]

    @pl.when(pl.program_id(0) == 0)
    def _():
        scale[...] = scale_of(tot_ref)

    for sub in range(x_ref.shape[1] // LANES):
        at = lanes_of(sub)
        normed = x_ref[:, at].astype(f32) * scale[...]
        u_ref[:, at] = (gate_ref[:, at].astype(f32) * normed).astype(bf16)


def behind_block(taps, own_ref, halo_ref, sub, masks):
    at = lanes_of(sub)
    signal = jnp.concatenate([halo_ref[:, at], own_ref[:, at]], axis=0)
    return filtered_block(taps[groups_of(sub)], signal, masks)


def flipped_taps(taps_ref):
    return jnp.dot(taps_ref[...], lag_flip(taps_ref.shape[1]), preferred_element_type=f32)


def forward_kernel(taps_ref, own_ref, halo_ref, gate_ref, *rest):
    z_ref, x_ref, ssq_ref, acc_ref = rest[-4:]
    step = pl.program_id(0)

    @pl.when(step == 0)
    def _():
        acc_ref[...] = jnp.zeros_like(acc_ref)

    taps = flipped_taps(taps_ref)
    masks = band_masks(HEIGHT, taps.shape[1], True)
    for sub in range(own_ref.shape[1] // LANES):
        at = lanes_of(sub)
        z = behind_block(taps, own_ref, halo_ref, sub, masks)
        z_ref[:, at] = z.astype(bf16)
        x = (gate_ref[:, at].astype(f32) * z).astype(bf16)
        x_ref[:, at] = x
        values = x.astype(f32)
        acc_ref[...] += values * values

    @pl.when(step == pl.num_programs(0) - 1)
    def _():
        ssq_ref[...] = lane_sums(acc_ref[...])


def last_forward_kernel(taps_ref, own_ref, halo_ref, top_ref, bottom_ref, *rest):
    out_ref = rest[-1]
    taps = flipped_taps(taps_ref)
    masks = band_masks(HEIGHT, taps.shape[1], True)
    for sub in range(own_ref.shape[1] // LANES):
        at = lanes_of(sub)
        z = behind_block(taps, own_ref, halo_ref, sub, masks)
        gradient = jnp.concatenate([top_ref[:, at], bottom_ref[:, at]], axis=0).astype(f32)
        out_ref[:, at] = (gradient * z).astype(bf16)


def gate_kernel(top_ref, bottom_ref, gate_ref, *rest):
    gz_ref = rest[-1]
    half = top_ref.shape[0]
    gz_ref[:half] = (top_ref[...].astype(f32) * gate_ref[:half].astype(f32)).astype(bf16)
    gz_ref[half:] = (bottom_ref[...].astype(f32) * gate_ref[half:].astype(f32)).astype(bf16)


def backward_kernel(taps_ref, own_ref, halo_ref, tot_ref, x_ref, gate_ref, *rest):
    out_ref, gn_ref, inner_ref, scale, acc_ref = rest[-5:]
    step = pl.program_id(0)

    @pl.when(step == 0)
    def _():
        scale[...] = scale_of(tot_ref)
        acc_ref[...] = jnp.zeros_like(acc_ref)

    taps = taps_ref[...].astype(f32)
    masks = band_masks(HEIGHT, taps.shape[1], False)
    for sub in range(own_ref.shape[1] // LANES):
        at = lanes_of(sub)
        signal = jnp.concatenate([own_ref[:, at], halo_ref[:, at]], axis=0)
        gu = filtered_block(taps[groups_of(sub)], signal, masks)
        normed = x_ref[:, at].astype(f32) * scale[...]
        out_ref[:, at] = (gu * normed).astype(bf16)
        gn = gu * gate_ref[:, at].astype(f32)
        gn_ref[:, at] = gn.astype(bf16)
        acc_ref[...] += gn * normed

    @pl.when(step == pl.num_programs(0) - 1)
    def _():
        inner_ref[...] = lane_sums(acc_ref[...])


def input_gradient(gn_ref, x_ref, at, scale, mean):
    normed = x_ref[:, at].astype(f32) * scale[...]
    return (scale[...] * (gn_ref[:, at].astype(f32) - normed * mean[...])).astype(bf16)


def between_kernel(gn_ref, x_ref, tot_ref, inner_ref, z_ref, gate_ref, *rest):
    out_ref, gz_ref, scale, mean = rest[-4:]

    @pl.when(pl.program_id(0) == 0)
    def _():
        scale[...] = scale_of(tot_ref)
        mean[...] = down_rows(inner_ref[0:1, :] / D)

    for sub in range(x_ref.shape[1] // LANES):
        at = lanes_of(sub)
        gradient = input_gradient(gn_ref, x_ref, at, scale, mean).astype(f32)
        gz_ref[:, at] = (gate_ref[:, at].astype(f32) * gradient).astype(bf16)
        out_ref[:, at] = (gradient * z_ref[:, at].astype(f32)).astype(bf16)


def finish_kernel(gn_ref, x_ref, tot_ref, inner_ref, *rest):
    top_ref, bottom_ref, scale, mean = rest[-4:]
    half = top_ref.shape[0]

    @pl.when(pl.program_id(0) == 0)
    def _():
        scale[...] = scale_of(tot_ref)
        mean[...] = down_rows(inner_ref[0:1, :] / D)

    for sub in range(x_ref.shape[1] // LANES):
        at = lanes_of(sub)
        gradient = input_gradient(gn_ref, x_ref, at, scale, mean)
        top_ref[:, at] = gradient[:half]
        bottom_ref[:, at] = gradient[half:]


def fold_kernel(odd_ref, first_ref, second_ref, *rest):
    out_ref = rest[-1]
    half = first_ref.shape[0]
    odd = odd_ref[0]

    @pl.when(odd == 0)
    def _():
        out_ref[:half] = first_ref[...]
        out_ref[half:] = second_ref[...]

    @pl.when(odd != 0)
    def _():
        out_ref[:half] = second_ref[...]
        out_ref[half:] = first_ref[...]


def taps_kernel(seqs, *refs):
    per = 3
    ins, (out_ref, flipped) = refs[: per * seqs], refs[-2:]
    rows = ins[0].shape[0]
    half = rows // 2
    count = LANES // GROUP
    step = pl.program_id(0)

    owner = lax.broadcasted_iota(jnp.int32, (half, LANES), 1) // GROUP
    row = lax.broadcasted_iota(jnp.int32, (half, LANES), 0)
    col = lax.broadcasted_iota(jnp.int32, (half, LANES), 1)
    masks = [(owner == g).astype(bf16) for g in range(count)]
    blocks = ins[0].shape[1] // LANES
    found = []
    for sub in range(blocks):
        at = lanes_of(sub)
        grads = []
        signals = []
        for s in range(seqs):
            gz_ref, own_ref, halo_ref = ins[per * s : per * s + 3]
            grads += [gz_ref[:half, at], gz_ref[half:, at]]
            signal = jnp.concatenate([halo_ref[:, at], own_ref[:, at]], axis=0)
            signals.append(windows(signal, half))
        wide = jnp.concatenate(grads, axis=1)
        left = jnp.concatenate(
            [wide * jnp.concatenate([masks[g]] * len(grads), axis=1) for g in range(count)],
            axis=0,
        )
        products = lax.dot_general(
            left,
            jnp.concatenate(signals, axis=1),
            (((1,), (1,)), ((), ())),
            preferred_element_type=f32,
        )
        slabs = []
        for g in range(count):
            mine = products[g * half : (g + 1) * half]
            wheel = jnp.where(col > row, mine[:, :LANES], mine[:, LANES:])
            slab = wheel[:SUB]
            for a in range(SUB, half, SUB):
                slab = slab + pltpu.roll(wheel[a : a + SUB], LANES - a, 1)
            slabs.append(slab)
        slabs = jnp.concatenate(slabs, axis=0)
        within = lax.rem(lax.broadcasted_iota(jnp.int32, slabs.shape, 0), SUB)
        for bit in (1, 2, 4):
            turned = pltpu.roll(slabs, LANES - bit, 1)
            slabs = jnp.where(within & bit != 0, turned, slabs)
        found.append(jnp.sum(slabs.reshape(count, SUB, LANES), axis=1))
    here = blocks * count
    flipped[pl.ds(pl.multiple_of(step * here, here), here), :] = jnp.concatenate(found, axis=0)

    @pl.when(step == pl.num_programs(0) - 1)
    def _():
        out_ref[...] = lax.dot_general(
            lag_flip(out_ref.shape[0]),
            flipped[...].astype(bf16),
            (((1,), (1,)), ((), ())),
            preferred_element_type=f32,
        )


def pack_kernel(*refs):
    out_ref = refs[-1]
    count, layers, lags = out_ref.shape[:3]
    for layer in range(layers):
        for part in range(count):
            out_ref[part, layer] = refs[layer][part * lags : (part + 1) * lags]


class Calls:
    def __init__(self, rows, width, taps, block):
        self.rows, self.width, self.taps, self.block = rows, width, taps, block
        self.steps = width // self.block
        self.latest = None

    def flat(self, array, s=None, layer=None, rows=None):
        rows = self.rows if rows is None else rows
        lead = tuple(i for i in (layer, s) if i is not None)
        spec = pl.BlockSpec(
            (None,) * len(lead) + (rows, self.block), lambda j, *_: lead + (0, j)
        )
        return array, spec

    def small(self, array=None, s=0):
        return array, pl.BlockSpec((SUB, self.rows), lambda j, *_: (s, 0))

    def filters(self, array, layer):
        count = self.block // GROUP
        return array, pl.BlockSpec((None, count, self.taps), lambda j, *_: (layer, j, 0))

    def square(self):
        return pltpu.VMEM((self.rows, self.rows), f32)

    def call(self, kernel, name, ins, outs, scratch=(), carry=None, prefetch=(), vmem=VMEM_LIMIT, after=()):
        operands = [a for a, _ in ins]
        in_specs = [b for _, b in ins]
        aliases = {}
        for array in (self.latest,) + tuple(after):
            if array is not None and array is not carry:
                operands.append(array)
                in_specs.append(pl.BlockSpec(memory_space=pl.ANY))
        if carry is not None:
            aliases = {len(prefetch) + len(operands): 0}
            operands.append(carry)
            in_specs.append(pl.BlockSpec(memory_space=pl.ANY))
        results = pl.pallas_call(
            kernel,
            name=name,
            out_shape=[jax.ShapeDtypeStruct(s, d) for s, d, _ in outs],
            grid_spec=pltpu.PrefetchScalarGridSpec(
                num_scalar_prefetch=len(prefetch),
                grid=(self.steps,),
                in_specs=in_specs,
                out_specs=[b for _, _, b in outs],
                scratch_shapes=list(scratch),
            ),
            input_output_aliases=aliases,
            compiler_params=pltpu.CompilerParams(
                dimension_semantics=("arbitrary",), vmem_limit_bytes=vmem
            ),
            cost_estimate=pl.CostEstimate(
                flops=1, bytes_accessed=1, transcendentals=0
            ),
        )(*prefetch, *operands)
        self.latest = results[-1]
        return results


def shifted(value, steps):
    count = lax.axis_size("ctx")
    first, last = max(0, -steps), min(count, count - steps)
    return lax.ppermute(value, "ctx", [(r, r + steps) for r in range(first, last)])


def over_channels(value):
    if lax.axis_size("ch") == 2:
        return value + lax.ppermute(value, "ch", [(0, 1), (1, 0)])
    return lax.psum(value, "ch")


def owner_routes(count):
    blocks = [[], []]
    for block in range(2 * count):
        folded = block if block < count else 2 * count - 1 - block
        blocks[block % 2].append((folded, block // 2))
    return blocks


def local(activations, grad_in, gate_out, gate_in, filters):
    seqs, rows, width = activations.shape
    taps = filters.shape[2]
    assert rows == taps == LANES
    half = rows // 2
    last = LAYERS - 1
    c = Calls(rows, width, taps, min(BLOCK, width))
    early = Calls(rows, width, taps, width)
    one = ((rows, width), bf16, c.flat(None)[1])
    part = ((half, width), bf16, c.flat(None, rows=half)[1])
    vector = ((SUB, rows), f32, c.small()[1])
    whole = (gate_out.shape, bf16)
    routes = owner_routes(lax.axis_size("ctx"))
    odd = lax.rem(lax.axis_index("ctx"), 2)

    def table():
        return [[None] * seqs for _ in range(LAYERS)]

    x, z, u, u_halo, tot = table(), table(), table(), table(), table()
    gz, gz_halo, gn, inner = table(), table(), table(), table()
    done = {"out": None, "in": None, "fold": None}
    found = [None] * LAYERS
    returned = [[None, None] for _ in range(seqs)]
    arrived = [None, None]

    def squares():
        (ssq,) = early.call(
            squares_kernel, "squares",
            [(activations, pl.BlockSpec((seqs, rows, width), lambda j: (0, 0, 0)))],
            [((seqs * SUB, rows), f32, pl.BlockSpec((seqs * SUB, rows), lambda j: (0, 0)))],
            [pltpu.VMEM((seqs, rows, rows), f32)], vmem=VMEM_MOST,
        )
        total = over_channels(ssq)
        for s in range(seqs):
            x[0][s] = c.flat(activations, s)
            tot[0][s] = c.small(total, s)

    def first_input(s):
        (u[0][s],) = early.call(
            input_kernel, "input",
            [early.flat(activations, s), tot[0][s], early.flat(gate_in, s, 0)],
            [((rows, width), bf16, early.flat(None)[1])], [c.square()], vmem=VMEM_MOST,
        )
        u_halo[0][s] = shifted(u[0][s], 1)
        c.latest = early.latest

    def gated_input(layer, s):
        (u[layer][s],) = c.call(
            input_kernel, "input",
            [x[layer][s], tot[layer][s], c.flat(gate_in, s, layer)], [one], [c.square()],
        )
        u_halo[layer][s] = shifted(u[layer][s], 1)

    def arrive():
        for side in range(2):
            start = jnp.where(odd == side, 0, half)
            piece = lax.dynamic_slice_in_dim(grad_in, start, half, axis=1)
            arrived[side] = lax.ppermute(piece, "ctx", routes[side])

    def arrived_of(s):
        return [c.flat(arrived[side], s, rows=half) for side in range(2)]

    def forward(layer, s):
        z[layer][s], nx, ssq = c.call(
            forward_kernel, "forward",
            [c.filters(filters, layer), c.flat(u[layer][s]), c.flat(u_halo[layer][s]),
             c.flat(gate_out, s, layer)],
            [one, one, vector], [c.square()],
        )
        x[layer + 1][s] = c.flat(nx)
        tot[layer + 1][s] = c.small(over_channels(ssq))

    def last_forward(s):
        (done["out"],) = c.call(
            last_forward_kernel, "last_forward",
            [c.filters(filters, last), c.flat(u[last][s]), c.flat(u_halo[last][s])]
            + arrived_of(s),
            [whole + (c.flat(None, s, last)[1],)], carry=done["out"],
        )

    def first_gate(s):
        (gz[last][s],) = c.call(
            gate_kernel, "gate", arrived_of(s) + [c.flat(gate_out, s, last)], [one]
        )
        gz_halo[last][s] = shifted(gz[last][s], -1)

    def backward(layer, s):
        done["in"], gn[layer][s], found_inner = c.call(
            backward_kernel, "backward",
            [c.filters(filters, layer), c.flat(gz[layer][s]), c.flat(gz_halo[layer][s]),
             tot[layer][s], x[layer][s], c.flat(gate_in, s, layer)],
            [whole + (c.flat(None, s, layer)[1],), one, vector],
            [c.square()] * 2, carry=done["in"],
        )
        inner[layer][s] = c.small(over_channels(found_inner))

    def common(layer, s):
        return [c.flat(gn[layer][s]), x[layer][s], tot[layer][s], inner[layer][s]]

    def between(layer, s):
        done["out"], gz[layer - 1][s] = c.call(
            between_kernel, "between",
            common(layer, s) + [c.flat(z[layer - 1][s]), c.flat(gate_out, s, layer - 1)],
            [whole + (c.flat(None, s, layer - 1)[1],), one],
            [c.square()] * 2, carry=done["out"],
        )
        gz_halo[layer - 1][s] = shifted(gz[layer - 1][s], -1)

    def finish(s):
        halves = c.call(
            finish_kernel, "finish", common(0, s), [part, part], [c.square()] * 2
        )
        for side in range(2):
            back = [(d, r) for r, d in routes[side]]
            returned[s][side] = lax.ppermute(halves[side], "ctx", back)

    def taps_of(layer):
        ins = []
        for s in range(seqs):
            ins += [c.flat(gz[layer][s]), c.flat(u[layer][s]), c.flat(u_halo[layer][s])]
        groups = width // GROUP
        (found[layer],) = c.call(
            functools.partial(taps_kernel, seqs), "taps", ins,
            [((taps, groups), f32, pl.BlockSpec((taps, groups), lambda j: (0, 0)))],
            [pltpu.VMEM((groups, taps), f32)], after=returned[0],
        )

    def fold(s):
        (done["fold"],) = c.call(
            fold_kernel, "fold",
            [c.flat(returned[s][side], rows=half) for side in range(2)],
            [(activations.shape, bf16, c.flat(None, s)[1])],
            carry=done["fold"], prefetch=(odd.reshape(1).astype(jnp.int32),),
        )

    def pack():
        groups = width // GROUP
        count = lax.axis_size("ctx")
        shape = (count, LAYERS, taps // count, groups)
        spec = pl.BlockSpec((taps, groups), lambda: (0, 0))
        tokens = [returned[-1][0], returned[-1][1]]
        return pl.pallas_call(
            pack_kernel,
            name="pack",
            out_shape=jax.ShapeDtypeStruct(shape, f32),
            in_specs=[spec] * LAYERS + [pl.BlockSpec(memory_space=pl.ANY)] * len(tokens),
            out_specs=pl.BlockSpec(shape, lambda: (0, 0, 0, 0)),
        )(*found, *tokens)

    arrive()
    squares()
    for s in range(seqs):
        first_input(s)
    for layer in range(last):
        for s in range(seqs):
            forward(layer, s)
            if layer + 1 < last:
                gated_input(layer + 1, s)
        if layer == 0:
            for s in range(seqs):
                first_gate(s)
    for s in range(seqs):
        backward(last, s)
        between(last, s)
    for s in range(seqs):
        gated_input(last, s)
    for layer in reversed(range(1, last)):
        for s in range(seqs):
            backward(layer, s)
            between(layer, s)
    for s in range(seqs):
        last_forward(s)
    for s in range(seqs):
        backward(0, s)
        finish(s)
    for layer in reversed(range(LAYERS)):
        taps_of(layer)

    mine = lax.all_to_all(pack(), "ctx", split_axis=0, concat_axis=0, tiled=True)
    grad_filters = jnp.swapaxes(jnp.sum(mine, axis=0), 1, 2)
    for s in range(seqs):
        fold(s)
    return done["fold"], done["out"], done["in"], grad_filters


def solution(mesh):
    return jax.shard_map(
        local,
        mesh=mesh,
        in_specs=(
            P(None, "ctx", "ch"),
            P(None, "ctx", "ch"),
            P(None, None, "ctx", "ch"),
            P(None, None, "ctx", "ch"),
            P(None, "ch", None),
        ),
        out_specs=(
            P(None, "ctx", "ch"),
            P(None, None, "ctx", "ch"),
            P(None, None, "ctx", "ch"),
            P(None, "ch", "ctx"),
        ),
        check_vma=False,
    )
```

```python
import functools

import jax
import jax.numpy as jnp
from jax import lax
from jax.experimental import pallas as pl
from jax.experimental.pallas import tpu as pltpu
from jax.sharding import PartitionSpec as P

D = 8192
GROUP = 16
LAYERS = 3
EPS = 1e-06
LANES = 128
SUB = 8
BLOCK = 1024
HEIGHT = 32
VMEM_LIMIT = 28 * 1024 * 1024
VMEM_MOST = 60 * 1024 * 1024

f32 = jnp.float32
bf16 = jnp.bfloat16


def down_rows(row):
    count = row.shape[1]
    return jnp.broadcast_to(row, (count, count)).T


def lane_sums(acc):
    return jnp.broadcast_to(jnp.sum(acc.T, axis=0, keepdims=True), (SUB, acc.shape[0]))


def lag_flip(taps):
    row = lax.broadcasted_iota(jnp.int32, (taps, taps), 0)
    col = lax.broadcasted_iota(jnp.int32, (taps, taps), 1)
    return (lax.rem(row + col, taps) == 0).astype(bf16)


def one_hot(taps):
    row = lax.broadcasted_iota(jnp.int32, (taps, taps), 0)
    col = lax.broadcasted_iota(jnp.int32, (taps, taps), 1)
    return (row == col).astype(bf16)


def band_masks(height, taps, behind):
    row = lax.broadcasted_iota(jnp.int32, (height, taps), 0)
    col = lax.broadcasted_iota(jnp.int32, (height, taps), 1)
    first = (col > row) if behind else (col >= row)
    return jnp.concatenate(
        [jnp.where(first, 1.0, 0.0), jnp.where(first, 0.0, 1.0)], axis=1
    ).astype(bf16)


def band(taps_row, masks):
    height, taps = masks.shape[0], taps_row.shape[1]
    wheel = pltpu.roll(
        jnp.broadcast_to(taps_row, (height, taps)), 0, 1, stride=1, stride_axis=0
    ).astype(bf16)
    return jnp.concatenate([wheel, wheel], axis=1) * masks


def windows(signal, height):
    count = signal.shape[0] // 2 // height
    return jnp.concatenate(
        [signal]
        + [
            jnp.concatenate([signal[k * height :], signal[: k * height]], axis=0)
            for k in range(1, count)
        ],
        axis=1,
    )


def group_pick(stacked, height, sides):
    count = LANES // GROUP
    owner = lax.broadcasted_iota(jnp.int32, (height, LANES), 1) // GROUP
    parts = []
    for side in range(sides):
        at = lanes_of(side)
        picked = stacked[:height, at]
        for g in range(1, count):
            picked = jnp.where(owner == g, stacked[g * height : (g + 1) * height, at], picked)
        parts.append(picked)
    return jnp.concatenate(parts, axis=0)


def filtered_block(taps_rows, signal, masks):
    height = masks.shape[0]
    count = LANES // GROUP
    bands = jnp.concatenate([band(taps_rows[g : g + 1], masks) for g in range(count)], axis=0)
    stacked = jnp.dot(bands, windows(signal, height), preferred_element_type=f32)
    return group_pick(stacked, height, signal.shape[0] // 2 // height)


def lanes_of(index):
    return slice(index * LANES, (index + 1) * LANES)


def groups_of(index):
    count = LANES // GROUP
    return slice(index * count, (index + 1) * count)


def scale_of(total_ref):
    return down_rows(lax.rsqrt(total_ref[0:1, :] / D + EPS))


def squares_kernel(x_ref, ssq_ref, acc_ref):
    step = pl.program_id(0)

    @pl.when(step == 0)
    def _():
        acc_ref[...] = jnp.zeros_like(acc_ref)

    for s in range(x_ref.shape[0]):
        for sub in range(x_ref.shape[2] // LANES):
            values = x_ref[s, :, lanes_of(sub)].astype(f32)
            acc_ref[s] += values * values

    @pl.when(step == pl.num_programs(0) - 1)
    def _():
        for s in range(x_ref.shape[0]):
            ssq_ref[s * SUB : (s + 1) * SUB] = lane_sums(acc_ref[s])


def input_kernel(x_ref, tot_ref, gate_ref, *rest):
    u_ref, scale = rest[-2:]

    @pl.when(pl.program_id(0) == 0)
    def _():
        scale[...] = scale_of(tot_ref)

    for sub in range(x_ref.shape[1] // LANES):
        at = lanes_of(sub)
        normed = x_ref[:, at].astype(f32) * scale[...]
        u_ref[:, at] = (gate_ref[:, at].astype(f32) * normed).astype(bf16)


def behind_block(taps, own_ref, halo_ref, sub, masks):
    at = lanes_of(sub)
    signal = jnp.concatenate([halo_ref[:, at], own_ref[:, at]], axis=0)
    return filtered_block(taps[groups_of(sub)], signal, masks)


def flipped_taps(taps_ref):
    return jnp.dot(taps_ref[...], lag_flip(taps_ref.shape[1]), preferred_element_type=f32)


def forward_kernel(taps_ref, own_ref, halo_ref, gate_ref, *rest):
    z_ref, x_ref, ssq_ref, acc_ref = rest[-4:]
    step = pl.program_id(0)

    @pl.when(step == 0)
    def _():
        acc_ref[...] = jnp.zeros_like(acc_ref)

    taps = flipped_taps(taps_ref)
    masks = band_masks(HEIGHT, taps.shape[1], True)
    for sub in range(own_ref.shape[1] // LANES):
        at = lanes_of(sub)
        z = behind_block(taps, own_ref, halo_ref, sub, masks)
        z_ref[:, at] = z.astype(bf16)
        x = (gate_ref[:, at].astype(f32) * z).astype(bf16)
        x_ref[:, at] = x
        values = x.astype(f32)
        acc_ref[...] += values * values

    @pl.when(step == pl.num_programs(0) - 1)
    def _():
        ssq_ref[...] = lane_sums(acc_ref[...])


def last_forward_kernel(taps_ref, own_ref, halo_ref, top_ref, bottom_ref, *rest):
    out_ref = rest[-1]
    taps = flipped_taps(taps_ref)
    masks = band_masks(HEIGHT, taps.shape[1], True)
    for sub in range(own_ref.shape[1] // LANES):
        at = lanes_of(sub)
        z = behind_block(taps, own_ref, halo_ref, sub, masks)
        gradient = jnp.concatenate([top_ref[:, at], bottom_ref[:, at]], axis=0).astype(f32)
        out_ref[:, at] = (gradient * z).astype(bf16)


def gate_kernel(top_ref, bottom_ref, gate_ref, *rest):
    gz_ref = rest[-1]
    half = top_ref.shape[0]
    gz_ref[:half] = (top_ref[...].astype(f32) * gate_ref[:half].astype(f32)).astype(bf16)
    gz_ref[half:] = (bottom_ref[...].astype(f32) * gate_ref[half:].astype(f32)).astype(bf16)


def backward_kernel(taps_ref, own_ref, halo_ref, tot_ref, x_ref, gate_ref, *rest):
    out_ref, gn_ref, inner_ref, scale, acc_ref = rest[-5:]
    step = pl.program_id(0)

    @pl.when(step == 0)
    def _():
        scale[...] = scale_of(tot_ref)
        acc_ref[...] = jnp.zeros_like(acc_ref)

    taps = taps_ref[...].astype(f32)
    masks = band_masks(HEIGHT, taps.shape[1], False)
    for sub in range(own_ref.shape[1] // LANES):
        at = lanes_of(sub)
        signal = jnp.concatenate([own_ref[:, at], halo_ref[:, at]], axis=0)
        gu = filtered_block(taps[groups_of(sub)], signal, masks)
        normed = x_ref[:, at].astype(f32) * scale[...]
        out_ref[:, at] = (gu * normed).astype(bf16)
        gn = gu * gate_ref[:, at].astype(f32)
        gn_ref[:, at] = gn.astype(bf16)
        acc_ref[...] += gn * normed

    @pl.when(step == pl.num_programs(0) - 1)
    def _():
        inner_ref[...] = lane_sums(acc_ref[...])


def input_gradient(gn_ref, x_ref, at, scale, mean):
    normed = x_ref[:, at].astype(f32) * scale[...]
    return (scale[...] * (gn_ref[:, at].astype(f32) - normed * mean[...])).astype(bf16)


def between_kernel(gn_ref, x_ref, tot_ref, inner_ref, z_ref, gate_ref, *rest):
    out_ref, gz_ref, scale, mean = rest[-4:]

    @pl.when(pl.program_id(0) == 0)
    def _():
        scale[...] = scale_of(tot_ref)
        mean[...] = down_rows(inner_ref[0:1, :] / D)

    for sub in range(x_ref.shape[1] // LANES):
        at = lanes_of(sub)
        gradient = input_gradient(gn_ref, x_ref, at, scale, mean).astype(f32)
        gz_ref[:, at] = (gate_ref[:, at].astype(f32) * gradient).astype(bf16)
        out_ref[:, at] = (gradient * z_ref[:, at].astype(f32)).astype(bf16)


def finish_kernel(gn_ref, x_ref, tot_ref, inner_ref, *rest):
    top_ref, bottom_ref, scale, mean = rest[-4:]
    half = top_ref.shape[0]

    @pl.when(pl.program_id(0) == 0)
    def _():
        scale[...] = scale_of(tot_ref)
        mean[...] = down_rows(inner_ref[0:1, :] / D)

    for sub in range(x_ref.shape[1] // LANES):
        at = lanes_of(sub)
        gradient = input_gradient(gn_ref, x_ref, at, scale, mean)
        top_ref[:, at] = gradient[:half]
        bottom_ref[:, at] = gradient[half:]


def fold_kernel(odd_ref, first_ref, second_ref, *rest):
    out_ref = rest[-1]
    half = first_ref.shape[0]
    odd = odd_ref[0]

    @pl.when(odd == 0)
    def _():
        out_ref[:half] = first_ref[...]
        out_ref[half:] = second_ref[...]

    @pl.when(odd != 0)
    def _():
        out_ref[:half] = second_ref[...]
        out_ref[half:] = first_ref[...]


def split_kernel(odd_ref, rows_ref, *rest):
    first_ref, second_ref = rest[-2:]
    half = first_ref.shape[1]
    odd = odd_ref[0]

    @pl.when(odd == 0)
    def _():
        first_ref[...] = rows_ref[:, :half]
        second_ref[...] = rows_ref[:, half:]

    @pl.when(odd != 0)
    def _():
        first_ref[...] = rows_ref[:, half:]
        second_ref[...] = rows_ref[:, :half]


def taps_kernel(seqs, *refs):
    per = 3
    ins, (out_ref, sums) = refs[: per * seqs], refs[-2:]
    rows = ins[0].shape[0]
    half = rows // 2
    count = LANES // GROUP
    step = pl.program_id(0)

    owner = lax.broadcasted_iota(jnp.int32, (half, LANES), 1) // GROUP
    row = lax.broadcasted_iota(jnp.int32, (half, LANES), 0)
    col = lax.broadcasted_iota(jnp.int32, (half, LANES), 1)
    masks = [(owner == g).astype(bf16) for g in range(count)]
    blocks = ins[0].shape[1] // LANES
    found = []
    for sub in range(blocks):
        at = lanes_of(sub)
        inputs = []
        signals = []
        for s in range(seqs):
            u_ref, own_ref, halo_ref = ins[per * s : per * s + 3]
            inputs += [u_ref[:half, at], u_ref[half:, at]]
            signal = jnp.concatenate([own_ref[:, at], halo_ref[:, at]], axis=0)
            signals.append(windows(signal, half))
        wide = jnp.concatenate(inputs, axis=1)
        left = jnp.concatenate(
            [wide * jnp.concatenate([masks[g]] * len(inputs), axis=1) for g in range(count)],
            axis=0,
        )
        products = lax.dot_general(
            left,
            jnp.concatenate(signals, axis=1),
            (((1,), (1,)), ((), ())),
            preferred_element_type=f32,
        )
        slabs = []
        for g in range(count):
            mine = products[g * half : (g + 1) * half]
            wheel = jnp.where(col >= row, mine[:, :LANES], mine[:, LANES:])
            slab = wheel[:SUB]
            for a in range(SUB, half, SUB):
                slab = slab + pltpu.roll(wheel[a : a + SUB], LANES - a, 1)
            slabs.append(slab)
        slabs = jnp.concatenate(slabs, axis=0)
        within = lax.rem(lax.broadcasted_iota(jnp.int32, slabs.shape, 0), SUB)
        for bit in (1, 2, 4):
            turned = pltpu.roll(slabs, LANES - bit, 1)
            slabs = jnp.where(within & bit != 0, turned, slabs)
        found.append(jnp.sum(slabs.reshape(count, SUB, LANES), axis=1))
    here = blocks * count
    sums[pl.ds(pl.multiple_of(step * here, here), here), :] = jnp.concatenate(found, axis=0)

    @pl.when(step == pl.num_programs(0) - 1)
    def _():
        out_ref[...] = lax.dot_general(
            one_hot(out_ref.shape[0]),
            sums[...].astype(bf16),
            (((1,), (1,)), ((), ())),
            preferred_element_type=f32,
        )


def pack_kernel(*refs):
    out_ref = refs[-1]
    count, layers, lags = out_ref.shape[:3]
    for layer in range(layers):
        for part in range(count):
            out_ref[part, layer] = refs[layer][part * lags : (part + 1) * lags]


class Calls:
    def __init__(self, rows, width, taps, block):
        self.rows, self.width, self.taps, self.block = rows, width, taps, block
        self.steps = width // self.block
        self.latest = None

    def flat(self, array, s=None, layer=None, rows=None):
        rows = self.rows if rows is None else rows
        lead = tuple(i for i in (layer, s) if i is not None)
        spec = pl.BlockSpec(
            (None,) * len(lead) + (rows, self.block), lambda j, *_: lead + (0, j)
        )
        return array, spec

    def small(self, array=None, s=0):
        return array, pl.BlockSpec((SUB, self.rows), lambda j, *_: (s, 0))

    def filters(self, array, layer):
        count = self.block // GROUP
        return array, pl.BlockSpec((None, count, self.taps), lambda j, *_: (layer, j, 0))

    def square(self):
        return pltpu.VMEM((self.rows, self.rows), f32)

    def call(self, kernel, name, ins, outs, scratch=(), carry=None, prefetch=(), vmem=VMEM_LIMIT, after=()):
        operands = [a for a, _ in ins]
        in_specs = [b for _, b in ins]
        aliases = {}
        for array in (self.latest,) + tuple(after):
            if array is not None and array is not carry:
                operands.append(array)
                in_specs.append(pl.BlockSpec(memory_space=pl.ANY))
        if carry is not None:
            aliases = {len(prefetch) + len(operands): 0}
            operands.append(carry)
            in_specs.append(pl.BlockSpec(memory_space=pl.ANY))
        results = pl.pallas_call(
            kernel,
            name=name,
            out_shape=[jax.ShapeDtypeStruct(s, d) for s, d, _ in outs],
            grid_spec=pltpu.PrefetchScalarGridSpec(
                num_scalar_prefetch=len(prefetch),
                grid=(self.steps,),
                in_specs=in_specs,
                out_specs=[b for _, _, b in outs],
                scratch_shapes=list(scratch),
            ),
            input_output_aliases=aliases,
            compiler_params=pltpu.CompilerParams(
                dimension_semantics=("arbitrary",), vmem_limit_bytes=vmem
            ),
            cost_estimate=pl.CostEstimate(
                flops=1, bytes_accessed=1, transcendentals=0
            ),
        )(*prefetch, *operands)
        self.latest = results[-1]
        return results


def shifted(value, steps):
    count = lax.axis_size("ctx")
    first, last = max(0, -steps), min(count, count - steps)
    return lax.ppermute(value, "ctx", [(r, r + steps) for r in range(first, last)])


def over_channels(value):
    if lax.axis_size("ch") == 2:
        return value + lax.ppermute(value, "ch", [(0, 1), (1, 0)])
    return lax.psum(value, "ch")


def owner_routes(count):
    blocks = [[], []]
    for block in range(2 * count):
        folded = block if block < count else 2 * count - 1 - block
        blocks[block % 2].append((folded, block // 2))
    return blocks


def local(activations, grad_in, gate_out, gate_in, filters):
    seqs, rows, width = activations.shape
    taps = filters.shape[2]
    assert rows == taps == LANES
    half = rows // 2
    last = LAYERS - 1
    c = Calls(rows, width, taps, min(BLOCK, width))
    early = Calls(rows, width, taps, width)
    one = ((rows, width), bf16, c.flat(None)[1])
    part = ((half, width), bf16, c.flat(None, rows=half)[1])
    vector = ((SUB, rows), f32, c.small()[1])
    whole = (gate_out.shape, bf16)
    routes = owner_routes(lax.axis_size("ctx"))
    odd = lax.rem(lax.axis_index("ctx"), 2)

    def table():
        return [[None] * seqs for _ in range(LAYERS)]

    x, z, u, u_halo, tot = table(), table(), table(), table(), table()
    gz, gz_halo, gn, inner = table(), table(), table(), table()
    done = {"out": None, "in": None, "fold": None}
    found = [None] * LAYERS
    returned = [[None, None] for _ in range(seqs)]
    arrived = [None, None]

    def squares():
        (ssq,) = early.call(
            squares_kernel, "squares",
            [(activations, pl.BlockSpec((seqs, rows, width), lambda j: (0, 0, 0)))],
            [((seqs * SUB, rows), f32, pl.BlockSpec((seqs * SUB, rows), lambda j: (0, 0)))],
            [pltpu.VMEM((seqs, rows, rows), f32)], vmem=VMEM_MOST,
        )
        total = over_channels(ssq)
        for s in range(seqs):
            x[0][s] = c.flat(activations, s)
            tot[0][s] = c.small(total, s)

    def first_input(s):
        (u[0][s],) = early.call(
            input_kernel, "input",
            [early.flat(activations, s), tot[0][s], early.flat(gate_in, s, 0)],
            [((rows, width), bf16, early.flat(None)[1])], [c.square()], vmem=VMEM_MOST,
        )
        u_halo[0][s] = shifted(u[0][s], 1)
        c.latest = early.latest

    def gated_input(layer, s):
        (u[layer][s],) = c.call(
            input_kernel, "input",
            [x[layer][s], tot[layer][s], c.flat(gate_in, s, layer)], [one], [c.square()],
        )
        u_halo[layer][s] = shifted(u[layer][s], 1)

    def arrive():
        spec = pl.BlockSpec((seqs, half, c.block), lambda j, *_: (0, 0, j))
        pieces = c.call(
            split_kernel, "split",
            [(grad_in, pl.BlockSpec((seqs, rows, c.block), lambda j, *_: (0, 0, j)))],
            [((seqs, half, width), bf16, spec)] * 2,
            prefetch=(odd.reshape(1).astype(jnp.int32),),
        )
        for side in range(2):
            arrived[side] = lax.ppermute(pieces[side], "ctx", routes[side])

    def arrived_of(s):
        return [c.flat(arrived[side], s, rows=half) for side in range(2)]

    def forward(layer, s):
        z[layer][s], nx, ssq = c.call(
            forward_kernel, "forward",
            [c.filters(filters, layer), c.flat(u[layer][s]), c.flat(u_halo[layer][s]),
             c.flat(gate_out, s, layer)],
            [one, one, vector], [c.square()],
        )
        x[layer + 1][s] = c.flat(nx)
        tot[layer + 1][s] = c.small(over_channels(ssq))

    def last_forward(s):
        (done["out"],) = c.call(
            last_forward_kernel, "last_forward",
            [c.filters(filters, last), c.flat(u[last][s]), c.flat(u_halo[last][s])]
            + arrived_of(s),
            [whole + (c.flat(None, s, last)[1],)], carry=done["out"],
        )

    def first_gate(s):
        (gz[last][s],) = c.call(
            gate_kernel, "gate", arrived_of(s) + [c.flat(gate_out, s, last)], [one]
        )
        gz_halo[last][s] = shifted(gz[last][s], -1)

    def backward(layer, s):
        done["in"], gn[layer][s], found_inner = c.call(
            backward_kernel, "backward",
            [c.filters(filters, layer), c.flat(gz[layer][s]), c.flat(gz_halo[layer][s]),
             tot[layer][s], x[layer][s], c.flat(gate_in, s, layer)],
            [whole + (c.flat(None, s, layer)[1],), one, vector],
            [c.square()] * 2, carry=done["in"],
        )
        inner[layer][s] = c.small(over_channels(found_inner))

    def common(layer, s):
        return [c.flat(gn[layer][s]), x[layer][s], tot[layer][s], inner[layer][s]]

    def between(layer, s):
        done["out"], gz[layer - 1][s] = c.call(
            between_kernel, "between",
            common(layer, s) + [c.flat(z[layer - 1][s]), c.flat(gate_out, s, layer - 1)],
            [whole + (c.flat(None, s, layer - 1)[1],), one],
            [c.square()] * 2, carry=done["out"],
        )
        gz_halo[layer - 1][s] = shifted(gz[layer - 1][s], -1)

    def finish(s):
        halves = c.call(
            finish_kernel, "finish", common(0, s), [part, part], [c.square()] * 2
        )
        for side in range(2):
            back = [(d, r) for r, d in routes[side]]
            returned[s][side] = lax.ppermute(halves[side], "ctx", back)

    def taps_of(layer):
        ins = []
        for s in range(seqs):
            ins += [c.flat(u[layer][s]), c.flat(gz[layer][s]), c.flat(gz_halo[layer][s])]
        groups = width // GROUP
        (found[layer],) = c.call(
            functools.partial(taps_kernel, seqs), "taps", ins,
            [((taps, groups), f32, pl.BlockSpec((taps, groups), lambda j: (0, 0)))],
            [pltpu.VMEM((groups, taps), f32)], after=() if layer else returned[0],
        )

    def fold(s):
        (done["fold"],) = c.call(
            fold_kernel, "fold",
            [c.flat(returned[s][side], rows=half) for side in range(2)],
            [(activations.shape, bf16, c.flat(None, s)[1])],
            carry=done["fold"], prefetch=(odd.reshape(1).astype(jnp.int32),),
        )

    def pack():
        groups = width // GROUP
        count = lax.axis_size("ctx")
        shape = (count, LAYERS, taps // count, groups)
        spec = pl.BlockSpec((taps, groups), lambda: (0, 0))
        tokens = [returned[-1][0], returned[-1][1]]
        return pl.pallas_call(
            pack_kernel,
            name="pack",
            out_shape=jax.ShapeDtypeStruct(shape, f32),
            in_specs=[spec] * LAYERS + [pl.BlockSpec(memory_space=pl.ANY)] * len(tokens),
            out_specs=pl.BlockSpec(shape, lambda: (0, 0, 0, 0)),
        )(*found, *tokens)

    squares()
    for s in range(seqs):
        first_input(s)
    for layer in range(last):
        for s in range(seqs):
            forward(layer, s)
            if layer + 1 < last:
                gated_input(layer + 1, s)
            if layer == 0 and s == 0:
                arrive()
    for s in range(seqs):
        first_gate(s)
    for s in range(seqs):
        backward(last, s)
        between(last, s)
    for s in range(seqs):
        gated_input(last, s)
    taps_of(last)
    for layer in reversed(range(1, last)):
        for s in range(seqs):
            backward(layer, s)
            between(layer, s)
        taps_of(layer)
    for s in range(seqs):
        last_forward(s)
    for s in range(seqs):
        backward(0, s)
        finish(s)
    taps_of(0)

    mine = lax.all_to_all(pack(), "ctx", split_axis=0, concat_axis=0, tiled=True)
    grad_filters = jnp.swapaxes(jnp.sum(mine, axis=0), 1, 2)
    for s in range(seqs):
        fold(s)
    return done["fold"], done["out"], done["in"], grad_filters


def solution(mesh):
    return jax.shard_map(
        local,
        mesh=mesh,
        in_specs=(
            P(None, "ctx", "ch"),
            P(None, "ctx", "ch"),
            P(None, None, "ctx", "ch"),
            P(None, None, "ctx", "ch"),
            P(None, "ch", None),
        ),
        out_specs=(
            P(None, "ctx", "ch"),
            P(None, None, "ctx", "ch"),
            P(None, None, "ctx", "ch"),
            P(None, "ch", "ctx"),
        ),
        check_vma=False,
    )
```

```python
import functools

import jax
import jax.numpy as jnp
from jax import lax
from jax.experimental import pallas as pl
from jax.experimental.pallas import tpu as pltpu
from jax.sharding import PartitionSpec as P

D = 8192
GROUP = 16
LAYERS = 3
EPS = 1e-06
LANES = 128
SUB = 8
BLOCK = 1024
HEIGHT = 32
VMEM_LIMIT = 28 * 1024 * 1024
VMEM_MOST = 60 * 1024 * 1024

f32 = jnp.float32
bf16 = jnp.bfloat16


def down_rows(row):
    count = row.shape[1]
    return jnp.broadcast_to(row, (count, count)).T


def lane_sums(acc):
    return jnp.broadcast_to(jnp.sum(acc.T, axis=0, keepdims=True), (SUB, acc.shape[0]))


def lag_flip(taps):
    row = lax.broadcasted_iota(jnp.int32, (taps, taps), 0)
    col = lax.broadcasted_iota(jnp.int32, (taps, taps), 1)
    return (lax.rem(row + col, taps) == 0).astype(bf16)


def one_hot(taps):
    row = lax.broadcasted_iota(jnp.int32, (taps, taps), 0)
    col = lax.broadcasted_iota(jnp.int32, (taps, taps), 1)
    return (row == col).astype(bf16)


def band_masks(height, taps, behind):
    row = lax.broadcasted_iota(jnp.int32, (height, taps), 0)
    col = lax.broadcasted_iota(jnp.int32, (height, taps), 1)
    first = (col > row) if behind else (col >= row)
    return jnp.concatenate(
        [jnp.where(first, 1.0, 0.0), jnp.where(first, 0.0, 1.0)], axis=1
    ).astype(bf16)


def band(taps_row, masks):
    height, taps = masks.shape[0], taps_row.shape[1]
    wheel = pltpu.roll(
        jnp.broadcast_to(taps_row, (height, taps)), 0, 1, stride=1, stride_axis=0
    ).astype(bf16)
    return jnp.concatenate([wheel, wheel], axis=1) * masks


def windows(signal, height):
    count = signal.shape[0] // 2 // height
    return jnp.concatenate(
        [signal]
        + [
            jnp.concatenate([signal[k * height :], signal[: k * height]], axis=0)
            for k in range(1, count)
        ],
        axis=1,
    )


def group_pick(stacked, height, sides):
    count = LANES // GROUP
    owner = lax.broadcasted_iota(jnp.int32, (height, LANES), 1) // GROUP
    parts = []
    for side in range(sides):
        at = lanes_of(side)
        picked = stacked[:height, at]
        for g in range(1, count):
            picked = jnp.where(owner == g, stacked[g * height : (g + 1) * height, at], picked)
        parts.append(picked)
    return jnp.concatenate(parts, axis=0)


def filtered_block(taps_rows, signal, masks):
    height = masks.shape[0]
    count = LANES // GROUP
    bands = jnp.concatenate([band(taps_rows[g : g + 1], masks) for g in range(count)], axis=0)
    stacked = jnp.dot(bands, windows(signal, height), preferred_element_type=f32)
    return group_pick(stacked, height, signal.shape[0] // 2 // height)


def lanes_of(index):
    return slice(index * LANES, (index + 1) * LANES)


def groups_of(index):
    count = LANES // GROUP
    return slice(index * count, (index + 1) * count)


def scale_of(total_ref):
    return down_rows(lax.rsqrt(total_ref[0:1, :] / D + EPS))


def squares_kernel(x_ref, ssq_ref, acc_ref):
    step = pl.program_id(0)

    @pl.when(step == 0)
    def _():
        acc_ref[...] = jnp.zeros_like(acc_ref)

    for s in range(x_ref.shape[0]):
        for sub in range(x_ref.shape[2] // LANES):
            values = x_ref[s, :, lanes_of(sub)].astype(f32)
            acc_ref[s] += values * values

    @pl.when(step == pl.num_programs(0) - 1)
    def _():
        for s in range(x_ref.shape[0]):
            ssq_ref[s * SUB : (s + 1) * SUB] = lane_sums(acc_ref[s])


def input_kernel(x_ref, tot_ref, gate_ref, *rest):
    u_ref, scale = rest[-2:]

    @pl.when(pl.program_id(0) == 0)
    def _():
        scale[...] = scale_of(tot_ref)

    for sub in range(x_ref.shape[1] // LANES):
        at = lanes_of(sub)
        normed = x_ref[:, at].astype(f32) * scale[...]
        u_ref[:, at] = (gate_ref[:, at].astype(f32) * normed).astype(bf16)


def behind_block(taps, own_ref, halo_ref, sub, masks):
    at = lanes_of(sub)
    signal = jnp.concatenate([halo_ref[:, at], own_ref[:, at]], axis=0)
    return filtered_block(taps[groups_of(sub)], signal, masks)


def flipped_taps(taps_ref):
    return jnp.dot(taps_ref[...], lag_flip(taps_ref.shape[1]), preferred_element_type=f32)


def forward_kernel(taps_ref, own_ref, halo_ref, gate_ref, *rest):
    z_ref, x_ref, ssq_ref, acc_ref = rest[-4:]
    step = pl.program_id(0)

    @pl.when(step == 0)
    def _():
        acc_ref[...] = jnp.zeros_like(acc_ref)

    taps = flipped_taps(taps_ref)
    masks = band_masks(HEIGHT, taps.shape[1], True)
    for sub in range(own_ref.shape[1] // LANES):
        at = lanes_of(sub)
        z = behind_block(taps, own_ref, halo_ref, sub, masks)
        z_ref[:, at] = z.astype(bf16)
        x = (gate_ref[:, at].astype(f32) * z).astype(bf16)
        x_ref[:, at] = x
        values = x.astype(f32)
        acc_ref[...] += values * values

    @pl.when(step == pl.num_programs(0) - 1)
    def _():
        ssq_ref[...] = lane_sums(acc_ref[...])


def last_forward_kernel(taps_ref, own_ref, halo_ref, top_ref, bottom_ref, *rest):
    out_ref = rest[-1]
    taps = flipped_taps(taps_ref)
    masks = band_masks(HEIGHT, taps.shape[1], True)
    for sub in range(own_ref.shape[1] // LANES):
        at = lanes_of(sub)
        z = behind_block(taps, own_ref, halo_ref, sub, masks)
        gradient = jnp.concatenate([top_ref[:, at], bottom_ref[:, at]], axis=0).astype(f32)
        out_ref[:, at] = (gradient * z).astype(bf16)


def gate_kernel(top_ref, bottom_ref, gate_ref, *rest):
    gz_ref = rest[-1]
    half = top_ref.shape[0]
    gz_ref[:half] = (top_ref[...].astype(f32) * gate_ref[:half].astype(f32)).astype(bf16)
    gz_ref[half:] = (bottom_ref[...].astype(f32) * gate_ref[half:].astype(f32)).astype(bf16)


def backward_kernel(taps_ref, own_ref, halo_ref, tot_ref, x_ref, gate_ref, *rest):
    out_ref, gn_ref, inner_ref, scale, acc_ref = rest[-5:]
    step = pl.program_id(0)

    @pl.when(step == 0)
    def _():
        scale[...] = scale_of(tot_ref)
        acc_ref[...] = jnp.zeros_like(acc_ref)

    taps = taps_ref[...].astype(f32)
    masks = band_masks(HEIGHT, taps.shape[1], False)
    for sub in range(own_ref.shape[1] // LANES):
        at = lanes_of(sub)
        signal = jnp.concatenate([own_ref[:, at], halo_ref[:, at]], axis=0)
        gu = filtered_block(taps[groups_of(sub)], signal, masks)
        normed = x_ref[:, at].astype(f32) * scale[...]
        out_ref[:, at] = (gu * normed).astype(bf16)
        gn = gu * gate_ref[:, at].astype(f32)
        gn_ref[:, at] = gn.astype(bf16)
        acc_ref[...] += gn * normed

    @pl.when(step == pl.num_programs(0) - 1)
    def _():
        inner_ref[...] = lane_sums(acc_ref[...])


def input_gradient(gn_ref, x_ref, at, scale, mean):
    normed = x_ref[:, at].astype(f32) * scale[...]
    return (scale[...] * (gn_ref[:, at].astype(f32) - normed * mean[...])).astype(bf16)


def between_kernel(gn_ref, x_ref, tot_ref, inner_ref, z_ref, gate_ref, *rest):
    out_ref, gz_ref, scale, mean = rest[-4:]

    @pl.when(pl.program_id(0) == 0)
    def _():
        scale[...] = scale_of(tot_ref)
        mean[...] = down_rows(inner_ref[0:1, :] / D)

    for sub in range(x_ref.shape[1] // LANES):
        at = lanes_of(sub)
        gradient = input_gradient(gn_ref, x_ref, at, scale, mean).astype(f32)
        gz_ref[:, at] = (gate_ref[:, at].astype(f32) * gradient).astype(bf16)
        out_ref[:, at] = (gradient * z_ref[:, at].astype(f32)).astype(bf16)


def finish_kernel(*refs):
    top_ref, bottom_ref, scales, means = refs[-4:]
    seqs, half = top_ref.shape[:2]
    per = 4
    ins = [refs[per * s : per * (s + 1)] for s in range(seqs)]

    @pl.when(pl.program_id(0) == 0)
    def _():
        for s, (_, _, tot_ref, inner_ref) in enumerate(ins):
            scales[s] = scale_of(tot_ref)
            means[s] = down_rows(inner_ref[0:1, :] / D)

    for s, (gn_ref, x_ref, _, _) in enumerate(ins):
        for sub in range(x_ref.shape[1] // LANES):
            at = lanes_of(sub)
            gradient = input_gradient(gn_ref, x_ref, at, scales.at[s], means.at[s])
            top_ref[s, :, at] = gradient[:half]
            bottom_ref[s, :, at] = gradient[half:]


def fold_kernel(odd_ref, first_ref, second_ref, *rest):
    out_ref = rest[-1]
    half = first_ref.shape[0]
    odd = odd_ref[0]

    @pl.when(odd == 0)
    def _():
        out_ref[:half] = first_ref[...]
        out_ref[half:] = second_ref[...]

    @pl.when(odd != 0)
    def _():
        out_ref[:half] = second_ref[...]
        out_ref[half:] = first_ref[...]


def split_kernel(odd_ref, rows_ref, *rest):
    first_ref, second_ref = rest[-2:]
    half = first_ref.shape[1]
    odd = odd_ref[0]

    @pl.when(odd == 0)
    def _():
        first_ref[...] = rows_ref[:, :half]
        second_ref[...] = rows_ref[:, half:]

    @pl.when(odd != 0)
    def _():
        first_ref[...] = rows_ref[:, half:]
        second_ref[...] = rows_ref[:, :half]


def taps_kernel(seqs, *refs):
    per = 3
    ins, (out_ref, sums) = refs[: per * seqs], refs[-2:]
    rows = ins[0].shape[0]
    half = rows // 2
    count = LANES // GROUP
    step = pl.program_id(0)

    owner = lax.broadcasted_iota(jnp.int32, (half, LANES), 1) // GROUP
    row = lax.broadcasted_iota(jnp.int32, (half, LANES), 0)
    col = lax.broadcasted_iota(jnp.int32, (half, LANES), 1)
    masks = [(owner == g).astype(bf16) for g in range(count)]
    blocks = ins[0].shape[1] // LANES
    found = []
    for sub in range(blocks):
        at = lanes_of(sub)
        inputs = []
        signals = []
        for s in range(seqs):
            u_ref, own_ref, halo_ref = ins[per * s : per * s + 3]
            inputs += [u_ref[:half, at], u_ref[half:, at]]
            signal = jnp.concatenate([own_ref[:, at], halo_ref[:, at]], axis=0)
            signals.append(windows(signal, half))
        wide = jnp.concatenate(inputs, axis=1)
        left = jnp.concatenate(
            [wide * jnp.concatenate([masks[g]] * len(inputs), axis=1) for g in range(count)],
            axis=0,
        )
        products = lax.dot_general(
            left,
            jnp.concatenate(signals, axis=1),
            (((1,), (1,)), ((), ())),
            preferred_element_type=f32,
        )
        slabs = []
        for g in range(count):
            mine = products[g * half : (g + 1) * half]
            wheel = jnp.where(col >= row, mine[:, :LANES], mine[:, LANES:])
            slab = wheel[:SUB]
            for a in range(SUB, half, SUB):
                slab = slab + pltpu.roll(wheel[a : a + SUB], LANES - a, 1)
            slabs.append(slab)
        slabs = jnp.concatenate(slabs, axis=0)
        within = lax.rem(lax.broadcasted_iota(jnp.int32, slabs.shape, 0), SUB)
        for bit in (1, 2, 4):
            turned = pltpu.roll(slabs, LANES - bit, 1)
            slabs = jnp.where(within & bit != 0, turned, slabs)
        found.append(jnp.sum(slabs.reshape(count, SUB, LANES), axis=1))
    here = blocks * count
    sums[pl.ds(pl.multiple_of(step * here, here), here), :] = jnp.concatenate(found, axis=0)

    @pl.when(step == pl.num_programs(0) - 1)
    def _():
        out_ref[...] = lax.dot_general(
            one_hot(out_ref.shape[0]),
            sums[...].astype(bf16),
            (((1,), (1,)), ((), ())),
            preferred_element_type=f32,
        )


def pack_kernel(*refs):
    out_ref = refs[-1]
    count, layers, lags = out_ref.shape[:3]
    for layer in range(layers):
        for part in range(count):
            out_ref[part, layer] = refs[layer][part * lags : (part + 1) * lags]


class Calls:
    def __init__(self, rows, width, taps, block):
        self.rows, self.width, self.taps, self.block = rows, width, taps, block
        self.steps = width // self.block
        self.latest = None

    def flat(self, array, s=None, layer=None, rows=None):
        rows = self.rows if rows is None else rows
        lead = tuple(i for i in (layer, s) if i is not None)
        spec = pl.BlockSpec(
            (None,) * len(lead) + (rows, self.block), lambda j, *_: lead + (0, j)
        )
        return array, spec

    def small(self, array=None, s=0):
        return array, pl.BlockSpec((SUB, self.rows), lambda j, *_: (s, 0))

    def filters(self, array, layer):
        count = self.block // GROUP
        return array, pl.BlockSpec((None, count, self.taps), lambda j, *_: (layer, j, 0))

    def square(self):
        return pltpu.VMEM((self.rows, self.rows), f32)

    def call(self, kernel, name, ins, outs, scratch=(), carry=None, prefetch=(), vmem=VMEM_LIMIT, after=()):
        operands = [a for a, _ in ins]
        in_specs = [b for _, b in ins]
        aliases = {}
        for array in (self.latest,) + tuple(after):
            if array is not None and array is not carry:
                operands.append(array)
                in_specs.append(pl.BlockSpec(memory_space=pl.ANY))
        if carry is not None:
            aliases = {len(prefetch) + len(operands): 0}
            operands.append(carry)
            in_specs.append(pl.BlockSpec(memory_space=pl.ANY))
        results = pl.pallas_call(
            kernel,
            name=name,
            out_shape=[jax.ShapeDtypeStruct(s, d) for s, d, _ in outs],
            grid_spec=pltpu.PrefetchScalarGridSpec(
                num_scalar_prefetch=len(prefetch),
                grid=(self.steps,),
                in_specs=in_specs,
                out_specs=[b for _, _, b in outs],
                scratch_shapes=list(scratch),
            ),
            input_output_aliases=aliases,
            compiler_params=pltpu.CompilerParams(
                dimension_semantics=("arbitrary",), vmem_limit_bytes=vmem
            ),
            cost_estimate=pl.CostEstimate(
                flops=1, bytes_accessed=1, transcendentals=0
            ),
        )(*prefetch, *operands)
        self.latest = results[-1]
        return results


def shifted(value, steps):
    count = lax.axis_size("ctx")
    first, last = max(0, -steps), min(count, count - steps)
    return lax.ppermute(value, "ctx", [(r, r + steps) for r in range(first, last)])


def over_channels(value):
    if lax.axis_size("ch") == 2:
        return value + lax.ppermute(value, "ch", [(0, 1), (1, 0)])
    return lax.psum(value, "ch")


def owner_routes(count):
    blocks = [[], []]
    for block in range(2 * count):
        folded = block if block < count else 2 * count - 1 - block
        blocks[block % 2].append((folded, block // 2))
    return blocks


def local(activations, grad_in, gate_out, gate_in, filters):
    seqs, rows, width = activations.shape
    taps = filters.shape[2]
    assert rows == taps == LANES
    half = rows // 2
    last = LAYERS - 1
    c = Calls(rows, width, taps, min(BLOCK, width))
    early = Calls(rows, width, taps, width)
    one = ((rows, width), bf16, c.flat(None)[1])
    vector = ((SUB, rows), f32, c.small()[1])
    whole = (gate_out.shape, bf16)
    routes = owner_routes(lax.axis_size("ctx"))
    odd = lax.rem(lax.axis_index("ctx"), 2)

    def table():
        return [[None] * seqs for _ in range(LAYERS)]

    x, z, u, u_halo, tot = table(), table(), table(), table(), table()
    gz, gz_halo, gn, inner = table(), table(), table(), table()
    done = {"out": None, "in": None, "fold": None}
    found = [None] * LAYERS
    returned = [None, None]
    arrived = [None, None]

    def squares():
        (ssq,) = early.call(
            squares_kernel, "squares",
            [(activations, pl.BlockSpec((seqs, rows, width), lambda j: (0, 0, 0)))],
            [((seqs * SUB, rows), f32, pl.BlockSpec((seqs * SUB, rows), lambda j: (0, 0)))],
            [pltpu.VMEM((seqs, rows, rows), f32)], vmem=VMEM_MOST,
        )
        total = over_channels(ssq)
        for s in range(seqs):
            x[0][s] = c.flat(activations, s)
            tot[0][s] = c.small(total, s)

    def first_input(s):
        (u[0][s],) = early.call(
            input_kernel, "input",
            [early.flat(activations, s), tot[0][s], early.flat(gate_in, s, 0)],
            [((rows, width), bf16, early.flat(None)[1])], [c.square()], vmem=VMEM_MOST,
        )
        u_halo[0][s] = shifted(u[0][s], 1)
        c.latest = early.latest

    def gated_input(layer, s):
        (u[layer][s],) = c.call(
            input_kernel, "input",
            [x[layer][s], tot[layer][s], c.flat(gate_in, s, layer)], [one], [c.square()],
        )
        u_halo[layer][s] = shifted(u[layer][s], 1)

    def arrive():
        spec = pl.BlockSpec((seqs, half, c.block), lambda j, *_: (0, 0, j))
        pieces = c.call(
            split_kernel, "split",
            [(grad_in, pl.BlockSpec((seqs, rows, c.block), lambda j, *_: (0, 0, j)))],
            [((seqs, half, width), bf16, spec)] * 2,
            prefetch=(odd.reshape(1).astype(jnp.int32),),
        )
        for side in range(2):
            arrived[side] = lax.ppermute(pieces[side], "ctx", routes[side])

    def arrived_of(s):
        return [c.flat(arrived[side], s, rows=half) for side in range(2)]

    def forward(layer, s):
        z[layer][s], nx, ssq = c.call(
            forward_kernel, "forward",
            [c.filters(filters, layer), c.flat(u[layer][s]), c.flat(u_halo[layer][s]),
             c.flat(gate_out, s, layer)],
            [one, one, vector], [c.square()],
        )
        x[layer + 1][s] = c.flat(nx)
        tot[layer + 1][s] = c.small(over_channels(ssq))

    def last_forward(s):
        (done["out"],) = c.call(
            last_forward_kernel, "last_forward",
            [c.filters(filters, last), c.flat(u[last][s]), c.flat(u_halo[last][s])]
            + arrived_of(s),
            [whole + (c.flat(None, s, last)[1],)], carry=done["out"],
        )

    def first_gate(s):
        (gz[last][s],) = c.call(
            gate_kernel, "gate", arrived_of(s) + [c.flat(gate_out, s, last)], [one]
        )
        gz_halo[last][s] = shifted(gz[last][s], -1)

    def backward(layer, s):
        done["in"], gn[layer][s], found_inner = c.call(
            backward_kernel, "backward",
            [c.filters(filters, layer), c.flat(gz[layer][s]), c.flat(gz_halo[layer][s]),
             tot[layer][s], x[layer][s], c.flat(gate_in, s, layer)],
            [whole + (c.flat(None, s, layer)[1],), one, vector],
            [c.square()] * 2, carry=done["in"],
        )
        inner[layer][s] = c.small(over_channels(found_inner))

    def common(layer, s):
        return [c.flat(gn[layer][s]), x[layer][s], tot[layer][s], inner[layer][s]]

    def between(layer, s):
        done["out"], gz[layer - 1][s] = c.call(
            between_kernel, "between",
            common(layer, s) + [c.flat(z[layer - 1][s]), c.flat(gate_out, s, layer - 1)],
            [whole + (c.flat(None, s, layer - 1)[1],), one],
            [c.square()] * 2, carry=done["out"],
        )
        gz_halo[layer - 1][s] = shifted(gz[layer - 1][s], -1)

    def finish():
        spec = pl.BlockSpec((seqs, half, c.block), lambda j, *_: (0, 0, j))
        halves = c.call(
            finish_kernel, "finish", [item for s in range(seqs) for item in common(0, s)],
            [((seqs, half, width), bf16, spec)] * 2,
            [pltpu.VMEM((seqs, rows, rows), f32)] * 2,
        )
        for side in range(2):
            back = [(d, r) for r, d in routes[side]]
            returned[side] = lax.ppermute(halves[side], "ctx", back)

    def taps_of(layer):
        ins = []
        for s in range(seqs):
            ins += [c.flat(u[layer][s]), c.flat(gz[layer][s]), c.flat(gz_halo[layer][s])]
        groups = width // GROUP
        (found[layer],) = c.call(
            functools.partial(taps_kernel, seqs), "taps", ins,
            [((taps, groups), f32, pl.BlockSpec((taps, groups), lambda j: (0, 0)))],
            [pltpu.VMEM((groups, taps), f32)],
        )

    def fold(s):
        (done["fold"],) = c.call(
            fold_kernel, "fold",
            [c.flat(returned[side], s, rows=half) for side in range(2)],
            [(activations.shape, bf16, c.flat(None, s)[1])],
            carry=done["fold"], prefetch=(odd.reshape(1).astype(jnp.int32),),
        )

    def pack():
        groups = width // GROUP
        count = lax.axis_size("ctx")
        shape = (count, LAYERS, taps // count, groups)
        spec = pl.BlockSpec((taps, groups), lambda: (0, 0))
        tokens = returned
        return pl.pallas_call(
            pack_kernel,
            name="pack",
            out_shape=jax.ShapeDtypeStruct(shape, f32),
            in_specs=[spec] * LAYERS + [pl.BlockSpec(memory_space=pl.ANY)] * len(tokens),
            out_specs=pl.BlockSpec(shape, lambda: (0, 0, 0, 0)),
        )(*found, *tokens)

    squares()
    for s in range(seqs):
        first_input(s)
    for layer in range(last):
        for s in range(seqs):
            forward(layer, s)
            if layer + 1 < last:
                gated_input(layer + 1, s)
            if layer == 0 and s == 0:
                arrive()
    for s in range(seqs):
        first_gate(s)
    for s in range(seqs):
        backward(last, s)
        between(last, s)
    for s in range(seqs):
        gated_input(last, s)
    taps_of(last)
    for layer in reversed(range(1, last)):
        for s in range(seqs):
            backward(layer, s)
            between(layer, s)
        taps_of(layer)
    for s in range(seqs):
        last_forward(s)
    for s in range(seqs):
        backward(0, s)
    finish()
    taps_of(0)

    mine = lax.all_to_all(pack(), "ctx", split_axis=0, concat_axis=0, tiled=True)
    grad_filters = jnp.swapaxes(jnp.sum(mine, axis=0), 1, 2)
    for s in range(seqs):
        fold(s)
    return done["fold"], done["out"], done["in"], grad_filters


def solution(mesh):
    return jax.shard_map(
        local,
        mesh=mesh,
        in_specs=(
            P(None, "ctx", "ch"),
            P(None, "ctx", "ch"),
            P(None, None, "ctx", "ch"),
            P(None, None, "ctx", "ch"),
            P(None, "ch", None),
        ),
        out_specs=(
            P(None, "ctx", "ch"),
            P(None, None, "ctx", "ch"),
            P(None, None, "ctx", "ch"),
            P(None, "ch", "ctx"),
        ),
        check_vma=False,
    )
```
